32 devices in a mesh: row: 8 (over y, x, core), col: 4 (over z).
Axes of the slice: x: 2, y: 2, z: 4, core: 2. Of those that a mesh axis runs over, the one named last changes fastest.
Arguments:
- before_scan: float32 [4, 2048, 4096], P(None, 'row', 'col'), may hold values from -40 to 40
- after_scan: float32 [4, 2048, 4096], P(None, 'row', 'col'), may hold values from -40 to 40
- drift_offsets: int32 [2, 4, 8, 4], P(None, None, 'row', 'col'), may hold values from -128 to 128, as said below
- drift_fractions: int32 [2, 4, 8, 4], P(None, None, 'row', 'col'), may hold values from 0 to 255
Outputs:
- band_field: float32 [4, 2048, 4096], P(None, 'row', 'col')
- slope_field: float32 [4, 2048, 4096], P(None, 'row', 'col')
- surface_params: float32 [2, 4], replicated
The draws below stay inside these ranges and needn't reach their ends.
Inputs may be any that keep to these rules, and one draw needn't show every extreme that they name: `drift_offsets`: for every scan and tile, the cells a tile reads (its own cells shifted by its offsets, widened by one row and column before and two after) lie inside the window. In every scan the first tile has offsets 128, 128 and the last tile minus 128, minus 128.
All inputs are finite; a program needn't handle non-finite values.
Results may differ from the reference program's by a relative error of at most 0.00014.
Values sent between devices are 32-bit elements; how exact they have to be, the bound alone decides.
A program may use at most 128 MiB of HBM per device.

```python
import math
import jax
import jax.numpy as jnp
from jax import lax

SCANS = 4
TR = 256
TC = 1024
LS = 5
SR = 4
LCUT = 1600
BLOCK = 16
DRIFT = 128
NR = 2048
NC = 4096
N_ROW = 8
N_COL = 4


wave_terms = 6


def scale_profile(row_power, col_power):
    row_frac = jnp.arange(NR, dtype=jnp.float32) / NR
    col_frac = jnp.arange(NC, dtype=jnp.float32) / NC
    return jnp.power(row_power, row_frac)[:, None] * jnp.power(col_power, col_frac)[None, :]


def rough_part(key):
    rough_noise = jnp.clip(jax.random.normal(key, (SCANS, NR, NC), jnp.float32), -4.0, 4.0)
    return 0.2 * rough_noise * scale_profile(10.0, 3.0)


def wave_part(key):
    subkeys = jax.random.split(key, 4)
    amplitude = jnp.clip(0.6 * jax.random.normal(subkeys[0], (SCANS, wave_terms), jnp.float32), -1.5, 1.5)
    row_waves = jax.random.uniform(subkeys[1], (SCANS, wave_terms), jnp.float32, -2.0, 2.0)
    col_waves = jax.random.uniform(subkeys[2], (SCANS, wave_terms), jnp.float32, -2.0, 2.0)
    phases = jax.random.uniform(subkeys[3], (SCANS, wave_terms), jnp.float32, 0.0, 2.0 * math.pi)
    row_frac = jnp.arange(NR, dtype=jnp.float32) / NR
    col_frac = jnp.arange(NC, dtype=jnp.float32) / NC
    waviness = jnp.zeros((SCANS, NR, NC), jnp.float32)
    for wave_index in range(wave_terms):
        argument = 2.0 * math.pi * (row_waves[:, wave_index, None, None] * row_frac[None, :, None] + col_waves[:, wave_index, None, None] * col_frac[None, None, :]) + phases[:, wave_index, None, None]
        waviness = waviness + amplitude[:, wave_index, None, None] * jnp.cos(argument)
    return waviness


def draw_before_scan(key, part):
    heights = rough_part(jax.random.fold_in(key, 1)) + wave_part(jax.random.fold_in(key, 2))
    return heights


def draw_after_scan(key, part):
    return rough_part(jax.random.fold_in(key, 3)) + wave_part(jax.random.fold_in(key, 4))


def draw_drift_offsets(key, part):
    drawn_values = jax.random.randint(jax.random.fold_in(key, 5), (2, SCANS, N_ROW, N_COL), -DRIFT, DRIFT + 1, dtype=jnp.int32)
    row_tile = jnp.arange(N_ROW, dtype=jnp.int32)[None, None, :, None]
    col_tile = jnp.arange(N_COL, dtype=jnp.int32)[None, None, None, :]
    full_shape = (1, SCANS, N_ROW, N_COL)
    row_low = jnp.broadcast_to(jnp.where(row_tile == 0, 1, -DRIFT), full_shape)
    row_high = jnp.broadcast_to(jnp.where(row_tile == N_ROW - 1, -2, DRIFT), full_shape)
    col_low = jnp.broadcast_to(jnp.where(col_tile == 0, 1, -DRIFT), full_shape)
    col_high = jnp.broadcast_to(jnp.where(col_tile == N_COL - 1, -2, DRIFT), full_shape)
    bounded = jnp.clip(drawn_values, jnp.concatenate([row_low, col_low], axis=0), jnp.concatenate([row_high, col_high], axis=0))
    bounded = bounded.at[:, :, 0, 0].set(DRIFT)
    return bounded.at[:, :, N_ROW - 1, N_COL - 1].set(-DRIFT).astype(jnp.int32)


def place_ends(result, key, low, top_value):
    extent = result.shape
    index_at = [jax.random.randint(jax.random.fold_in(key, axis), (), 0, extent[axis]) for axis in range(len(extent))]
    result = result.at[tuple(index_at)].set(low)
    longest = extent.index(max(extent))
    index_at[longest] = (index_at[longest] + 1) % extent[longest]
    return result.at[tuple(index_at)].set(top_value)


def setup_inputs(seed: int = 0) -> dict:
    splits = jax.random.split(jax.random.key(seed), 5)
    before_scan = draw_before_scan(jax.random.fold_in(splits[4], 71), 0)
    after_scan = draw_after_scan(jax.random.fold_in(splits[4], 71), 0)
    drift_offsets = draw_drift_offsets(jax.random.fold_in(splits[4], 71), 0)
    drift_fractions = place_ends(jax.random.randint(splits[3], (2, SCANS, N_ROW, N_COL), 0, 256), jax.random.fold_in(splits[3], 1), 0, 255).astype(jnp.int32)
    return dict(before_scan=before_scan, after_scan=after_scan, drift_offsets=drift_offsets, drift_fractions=drift_fractions)


ALPHA = math.sqrt(math.log(2.0) / math.pi)
SPACING = 0.5
EPSILON = 1e-06
HIGHEST = lax.Precision.HIGHEST

def cubic_weights(fraction):
    position = fraction.astype(jnp.float32) / 256.0
    square = position * position
    cube_term = square * position
    return (0.5 * (2.0 * square - cube_term - position), 0.5 * (3.0 * cube_term - 5.0 * square + 2.0), 0.5 * (4.0 * square - 3.0 * cube_term + position), 0.5 * (cube_term - square))

def interpolate(window, row_taps, col_taps):
    height = window.shape[0] - 3
    length = window.shape[1] - 3
    across = row_taps[0] * window[0:height] + row_taps[1] * window[1:height + 1] + row_taps[2] * window[2:height + 2] + row_taps[3] * window[3:height + 3]
    return col_taps[0] * across[:, 0:length] + col_taps[1] * across[:, 1:length + 1] + col_taps[2] * across[:, 2:length + 2] + col_taps[3] * across[:, 3:length + 3]

def resample(after_scan, drift_offsets, drift_fractions):
    margin = DRIFT + 2
    padded = jnp.pad(after_scan, ((0, 0), (margin, margin), (margin, margin)))
    scan_id = jnp.broadcast_to(jnp.arange(SCANS, dtype=jnp.int32)[:, None, None], (SCANS, N_ROW, N_COL))
    row_start = jnp.arange(N_ROW, dtype=jnp.int32)[None, :, None] * TR + (margin - 1) + drift_offsets[0]
    col_start = jnp.arange(N_COL, dtype=jnp.int32)[None, None, :] * TC + (margin - 1) + drift_offsets[1]
    row_taps = jnp.stack(cubic_weights(drift_fractions[0]), axis=-1).reshape(-1, 4)
    col_taps = jnp.stack(cubic_weights(drift_fractions[1]), axis=-1).reshape(-1, 4)

    def one_tile(scan_index, row_first, col_first, row_weights, col_weights):
        window = lax.dynamic_slice(padded, (scan_index, row_first, col_first), (1, TR + 3, TC + 3))[0]
        return interpolate(window, row_weights, col_weights)
    resampled = jax.vmap(one_tile)(scan_id.reshape(-1), row_start.reshape(-1).astype(jnp.int32), col_start.reshape(-1).astype(jnp.int32), row_taps, col_taps)
    resampled = resampled.reshape(SCANS, N_ROW, N_COL, TR, TC).transpose(0, 1, 3, 2, 4)
    return resampled.reshape(SCANS, NR, NC)

def short_taps():
    return [math.exp(-math.pi * (offset / (ALPHA * LS)) ** 2) for offset in range(-SR, SR + 1)]

def short_filter(surface):
    kernel_taps = short_taps()
    padded = jnp.pad(surface, ((0, 0), (0, 0), (SR, SR)))
    inside = jnp.pad(jnp.ones((NC,), jnp.float32), (SR, SR))
    summed = kernel_taps[0] * padded[:, :, 0:NC]
    weight = kernel_taps[0] * inside[0:NC]
    for offset in range(1, 2 * SR + 1):
        summed = summed + kernel_taps[offset] * padded[:, :, offset:offset + NC]
        weight = weight + kernel_taps[offset] * inside[offset:offset + NC]
    across = summed / weight
    padded = jnp.pad(across, ((0, 0), (SR, SR), (0, 0)))
    inside = jnp.pad(jnp.ones((NR,), jnp.float32), (SR, SR))
    summed = kernel_taps[0] * padded[:, 0:NR, :]
    weight = kernel_taps[0] * inside[0:NR]
    for offset in range(1, 2 * SR + 1):
        summed = summed + kernel_taps[offset] * padded[:, offset:offset + NR, :]
        weight = weight + kernel_taps[offset] * inside[offset:offset + NR]
    return summed / weight[:, None]

def coarse_means(surface):
    return surface.reshape(SCANS, NR // BLOCK, BLOCK, NC // BLOCK, BLOCK).mean(axis=(2, 4))

def gauss_block(source, target):
    distance = ((source[:, None] - target[None, :]) * BLOCK).astype(jnp.float32) / (ALPHA * LCUT)
    return jnp.exp(-math.pi * distance * distance)

def upsample_matrix(fine_index, coarse_index, coarse_count):
    numerator = 2 * fine_index + 1 - BLOCK
    lower_index = numerator // (2 * BLOCK)
    fraction = (numerator - lower_index * (2 * BLOCK)).astype(jnp.float32) / (2.0 * BLOCK)
    outside = (lower_index < 0) | (lower_index >= coarse_count - 1)
    fraction = jnp.where(outside, jnp.zeros_like(fraction), fraction)
    lower_index = jnp.clip(lower_index, 0, coarse_count - 1)
    first_part = (coarse_index[None, :] == lower_index[:, None]).astype(jnp.float32) * (1.0 - fraction)[:, None]
    second_part = (coarse_index[None, :] == (lower_index + 1)[:, None]).astype(jnp.float32) * fraction[:, None]
    return first_part + second_part

def slopes(surface):
    padded = jnp.pad(surface, ((0, 0), (1, 1), (1, 1)))
    column_index = jnp.arange(NC, dtype=jnp.int32)
    row_index = jnp.arange(NR, dtype=jnp.int32)
    column_mask = ((column_index >= 1) & (column_index <= NC - 2)).astype(jnp.float32)
    row_mask = ((row_index >= 1) & (row_index <= NR - 2)).astype(jnp.float32)
    along_cols = (padded[:, 1:-1, 2:] - padded[:, 1:-1, :-2]) / (2.0 * SPACING) * column_mask
    along_rows = (padded[:, 2:, 1:-1] - padded[:, :-2, 1:-1]) / (2.0 * SPACING) * row_mask[:, None]
    return along_cols * along_cols + along_rows * along_rows

def reference(before_scan, after_scan, drift_offsets, drift_fractions):
    shifted = resample(after_scan, drift_offsets, drift_fractions)
    difference = before_scan - shifted
    smooth = short_filter(difference)
    coarse = coarse_means(smooth)
    coarse_cols = jnp.arange(NC // BLOCK, dtype=jnp.int32)
    col_matrix = gauss_block(coarse_cols, coarse_cols)
    along = jnp.einsum('sak,kb->sab', coarse, col_matrix, precision=HIGHEST) / lax.optimization_barrier(jnp.sum(col_matrix, axis=0))
    coarse_rows = jnp.arange(NR // BLOCK, dtype=jnp.int32)
    row_matrix = gauss_block(coarse_rows, coarse_rows)
    wavy_coarse = jnp.einsum('ak,skb->sab', row_matrix, along, precision=HIGHEST) / lax.optimization_barrier(jnp.sum(row_matrix, axis=1))[:, None]
    row_up = upsample_matrix(jnp.arange(NR, dtype=jnp.int32), coarse_rows, NR // BLOCK)
    col_up = upsample_matrix(jnp.arange(NC, dtype=jnp.int32), coarse_cols, NC // BLOCK)
    row_mixed = jnp.einsum('pa,sab->spb', row_up, wavy_coarse, precision=HIGHEST)
    waviness = jnp.einsum('spb,qb->spq', row_mixed, col_up, precision=HIGHEST)
    band_field = smooth - waviness
    slope_field = slopes(band_field)
    height_sq = lax.optimization_barrier(jnp.sum(band_field * band_field, axis=(1, 2)))
    slope_sum = lax.optimization_barrier(jnp.sum(slope_field, axis=(1, 2)))
    surface_params = jnp.sqrt(jnp.stack([height_sq, slope_sum]) / (NR * NC) + EPSILON)
    return (band_field, slope_field, surface_params)
```

```python
import functools
import math

import jax
import jax.numpy as jnp
import numpy as np
from jax import lax
from jax.experimental import pallas as pl
from jax.experimental.pallas import tpu as pltpu
from jax.sharding import PartitionSpec as P

LS = 5
SR = 4
LCUT = 1600
BLOCK = 16
DRIFT = 128
EPSILON = 1e-06
ALPHA = math.sqrt(math.log(2.0) / math.pi)
TAPS = [math.exp(-math.pi * (k / (ALPHA * LS)) ** 2) for k in range(-SR, SR + 1)]
HALO = 136
LANES = 128
EDGE = 8
F32 = jnp.float32
BF16 = jnp.bfloat16
HIGHEST = lax.Precision.HIGHEST
MESH = pl.DeviceIdType.MESH
ANY = pl.BlockSpec(memory_space=pl.ANY)
VM = pl.BlockSpec(memory_space=pltpu.VMEM)
VMEM_LIMIT = 56 * 1024 * 1024


def short_matrix(count):
    index = np.arange(count)
    matrix = np.zeros((count, count), np.float64)
    for k in range(-SR, SR + 1):
        rows = index[(index + k >= 0) & (index + k < count)]
        matrix[rows, rows + k] = TAPS[k + SR]
    return matrix, matrix.sum(axis=1)


def coarse_table(count, tile, padded):
    parts = count // tile
    blocks = tile // BLOCK
    _, weight = short_matrix(count)
    table = np.zeros((parts, padded, tile), np.float64)
    for part in range(parts):
        for b in range(-1, blocks + 1):
            target = part * blocks + b
            if target < 0 or target >= count // BLOCK:
                continue
            for p in range(target * BLOCK, (target + 1) * BLOCK):
                for k in range(-SR, SR + 1):
                    source = p + k - part * tile
                    if 0 <= source < tile:
                        table[part, b + 1, source] += TAPS[k + SR] / weight[p] / BLOCK
    return table


def long_matrix(blocks):
    index = np.arange(blocks)
    distance = (index[:, None] - index[None, :]) * BLOCK / (ALPHA * LCUT)
    matrix = np.exp(-math.pi * distance * distance)
    return matrix / matrix.sum(axis=1, keepdims=True)


def upsample_rows(count, first, length):
    blocks = count // BLOCK
    result = np.zeros((length, blocks), np.float64)
    for n in range(length):
        p = first + n
        if p < 0 or p >= count:
            continue
        u = (2 * p + 1 - BLOCK) / (2 * BLOCK)
        i = math.floor(u)
        f = u - i
        if i < 0:
            i, f = 0, 0.0
        if i >= blocks - 1:
            i, f = blocks - 1, 0.0
        result[n, i] += 1 - f
        if f:
            result[n, i + 1] += f
    return result


def spread_table(count, tile, padded):
    parts, blocks = count // tile, tile // BLOCK
    total = count // BLOCK
    table = np.zeros((total, parts, padded), np.float64)
    matrix = long_matrix(total)
    for part in range(parts):
        for b in range(-1, blocks + 1):
            source = part * blocks + b
            if 0 <= source < total:
                table[:, part, b + 1] = matrix[:, source]
    return table


@functools.lru_cache(maxsize=None)
def tables(nr, nc, tr, tc):
    n_row, n_col = nr // tr, nc // tc
    br, bc = tr // BLOCK, tc // BLOCK
    pr = -(-(br + 2) // 8) * 8
    r_table = coarse_table(nr, tr, pr)
    c_table = coarse_table(nc, tc, LANES).transpose(0, 2, 1)
    col_spread = spread_table(nc, tc, LANES)
    hc = np.zeros((n_col, n_col, LANES, LANES))
    cu = np.zeros((n_col, LANES, tc + 2 * LANES))
    for part in range(n_col):
        for b in range(-1, bc + 1):
            target = part * bc + b
            if 0 <= target < nc // BLOCK:
                hc[part, :, :, b + 1] = col_spread[target]
        up = upsample_rows(nc, part * tc - LANES, tc + 2 * LANES)
        for b in range(-1, bc + 1):
            target = part * bc + b
            if 0 <= target < nc // BLOCK:
                cu[part, b + 1] = up[:, target]
    row_spread = spread_table(nr, tr, pr).reshape(nr // BLOCK, n_row * pr)
    ru = np.stack(
        [upsample_rows(nr, part * tr - EDGE, tr + 2 * EDGE) @ row_spread for part in range(n_row)]
    )
    _, row_weight = short_matrix(nr)
    _, col_weight = short_matrix(nc)
    rw = np.zeros((n_row, tr + 2 * EDGE, 1))
    cw = np.zeros((n_col, 1, tc + 2 * LANES))
    for part in range(n_row):
        for n in range(tr + 2 * EDGE):
            p = part * tr - EDGE + n
            if 0 <= p < nr:
                rw[part, n, 0] = 1.0 / row_weight[p]
    for part in range(n_col):
        for n in range(tc + 2 * LANES):
            q = part * tc - LANES + n
            if 0 <= q < nc:
                cw[part, 0, n] = 1.0 / col_weight[q]
    return [t.astype(np.float32) for t in (r_table, c_table, hc, cu, ru, rw, cw)]


def remote(src, dst, send, recv, device):
    return pltpu.make_async_remote_copy(
        src_ref=src, dst_ref=dst, send_sem=send, recv_sem=recv,
        device_id=device, device_id_type=MESH,
    )


def signal(barrier, device):
    pl.semaphore_signal(barrier, inc=1, device_id=device, device_id_type=MESH)


def neighbours(n_row, n_col):
    row, col = lax.axis_index("row"), lax.axis_index("col")
    found = {}
    for dr in (-1, 0, 1):
        for dc in (-1, 0, 1):
            if dr == 0 and dc == 0:
                continue
            r, c = row + dr, col + dc
            exists = (r >= 0) & (r < n_row) & (c >= 0) & (c < n_col)
            found[dr, dc] = (exists, (r, c))
    return found


def halo_kernel(n_row, n_col, after, extra, wide, slots, own_sem, send, recv, slot_send, slot_recv):
    scans, height, length = after.shape
    near = neighbours(n_row, n_col)
    barrier = pltpu.get_barrier_semaphore()
    count = jnp.int32(0)
    for exists, device in near.values():
        count += exists.astype(jnp.int32)

        @pl.when(exists)
        def _():
            signal(barrier, device)

    pl.semaphore_wait(barrier, count)
    low, high = HALO, HALO + height
    bands = {-1: (0, HALO), 0: (low, height), 1: (high, HALO)}
    mid = pl.ds(LANES, length)

    def row_copy(s, dr):
        src = pl.ds(height - HALO, HALO) if dr == 1 else pl.ds(0, HALO)
        dst = pl.ds(0, HALO) if dr == 1 else pl.ds(high, HALO)
        k = 0 if dr == 1 else 1
        return remote(
            after.at[s, src, :], wide.at[s, dst, mid], send.at[k, s], recv.at[k, s], near[dr, 0][1]
        )

    def col_copy(s, dc, band):
        start, rows = bands[band]
        k = 2 + (band + 1) * 2 + (0 if dc == 1 else 1)
        first = length - LANES if dc == 1 else 0
        if band == 0:
            src = after.at[s, :, pl.ds(first, LANES)]
        else:
            src = wide.at[s, pl.ds(start, rows), pl.ds(LANES + first, LANES)]
        dst = wide.at[s, pl.ds(start, rows), pl.ds(0 if dc == 1 else LANES + length, LANES)]
        return remote(src, dst, send.at[k, s], recv.at[k, s], near[0, dc][1])

    def slot_copy(dr, dc):
        k = (0 if dc == 1 else 3) + (1 - dr)
        return remote(extra, slots.at[k], slot_send.at[k], slot_recv.at[k], near[dr, dc][1])

    def when(pred, action):
        pl.when(pred)(action)

    for s in range(scans):
        for dr in (1, -1):
            when(near[dr, 0][0], row_copy(s, dr).start)
    for s in range(scans):
        for dc in (1, -1):
            when(near[0, dc][0], col_copy(s, dc, 0).start)
    own = pltpu.make_async_copy(after, wide.at[:, pl.ds(low, height), mid], own_sem)
    own.start()
    for dc in (1, -1):
        for dr in (-1, 0, 1):
            when(near[dr, dc][0], slot_copy(dr, dc).start)
    for s in range(scans):
        for dr in (1, -1):
            source = near[-dr, 0][0]
            when(source, row_copy(s, dr).wait_recv)
            for dc in (1, -1):
                when(source & near[0, dc][0], col_copy(s, dc, -dr).start)
    for s in range(scans):
        for dr in (1, -1):
            when(near[dr, 0][0], row_copy(s, dr).wait_send)
        for dc in (1, -1):
            for band in (-1, 0, 1):
                ok = jnp.bool_(True) if band == 0 else near[band, 0][0]
                when(ok & near[0, dc][0], col_copy(s, dc, band).wait_send)
                when(ok & near[0, -dc][0], col_copy(s, dc, band).wait_recv)
    for dc in (1, -1):
        for dr in (-1, 0, 1):
            when(near[dr, dc][0], slot_copy(dr, dc).wait_send)
            when(near[-dr, -dc][0], slot_copy(dr, dc).wait_recv)
    own.wait()


def split3(value):
    a = value.astype(BF16)
    rest = value - a.astype(F32)
    b = rest.astype(BF16)
    c = (rest - b.astype(F32)).astype(BF16)
    return a, b, c


def cubic(t):
    t2 = t * t
    t3 = t2 * t
    return (
        0.5 * (2.0 * t2 - t3 - t),
        0.5 * (3.0 * t3 - 5.0 * t2 + 2.0),
        0.5 * (4.0 * t2 - 3.0 * t3 + t),
        0.5 * (t3 - t2),
    )


def shift_kernel(place, offsets, fractions, wide, before, slots, r_tab, c_tab, diff, partial, edges, tail):
    s = pl.program_id(0)
    height, length = before.shape[1], before.shape[2]
    total = length + 3 * LANES
    dr, dc = offsets[0, s], offsets[1, s]
    rt = cubic(fractions[0, s].astype(F32) / 256.0)
    ct = cubic(fractions[1, s].astype(F32) / 256.0)
    blank = jnp.zeros((LANES - 16, height), F32)
    for j in range(3):
        block = jnp.concatenate([slots[3 + j, 0], blank, slots[j, 0]], axis=0)
        flipped = jnp.transpose(block)
        if j == 0:
            tail[0:HALO] = flipped[height - HALO :]
        elif j == 1:
            tail[HALO : HALO + height] = flipped
        else:
            tail[HALO + height :] = flipped[:HALO]
    turn = 2 * total - LANES - dc + 1
    turn = lax.rem(turn, total)
    start = HALO - 1 + dr
    rows = 32

    def step(r, carry):
        first = start + r * rows
        base = pl.multiple_of((first // 8) * 8, 8)
        off = first - base
        x = jnp.concatenate(
            [wide[0, pl.ds(base, rows + 16), :], tail[pl.ds(base, rows + 16), :]], axis=1
        )
        x = pltpu.roll(x, lax.rem(rows + 16 - off, rows + 16), 0)
        y = rt[0] * x[0:rows] + rt[1] * x[1 : rows + 1] + rt[2] * x[2 : rows + 2] + rt[3] * x[3 : rows + 3]
        y = pltpu.roll(y, turn, 1)
        z = ct[0] * y[:, 0:length]
        for b in range(1, 4):
            z = z + ct[b] * pltpu.roll(y, total - b, 1)[:, 0:length]
        here = pl.ds(pl.multiple_of(r * rows, rows), rows)
        diff[0, here, :] = before[0, here, :] - z
        return carry

    lax.fori_loop(0, height // rows, step, 0)
    d = diff[0]
    mixed = jnp.dot(r_tab[0], d, precision=HIGHEST, preferred_element_type=F32)
    partial[0] = jnp.dot(mixed, c_tab[0], precision=HIGHEST, preferred_element_type=F32)
    edges[0, 0:EDGE] = jnp.transpose(diff[0, :, 0:LANES])[0:EDGE]
    edges[0, EDGE:] = jnp.transpose(diff[0, :, length - LANES :])[LANES - EDGE :]


def gather_kernel(n_row, n_col, diff, partial, edges, hc, rows_out, corners, sides, spread, parts,
                  psend, precv, qsend, qrecv, nsend, nrecv):
    scans, height, length = diff.shape
    near = neighbours(n_row, n_col)
    row, col = lax.axis_index("row"), lax.axis_index("col")
    barrier = pltpu.get_barrier_semaphore()
    count = jnp.int32(n_row - 1 + n_col - 1)
    for k in range(1, n_col):
        signal(barrier, (row, lax.rem(col + k, n_col)))
    for k in range(1, n_row):
        signal(barrier, (lax.rem(row + k, n_row), col))
    for (dr, dc), (exists, device) in near.items():
        if dr and dc:
            count += exists.astype(jnp.int32)

            @pl.when(exists)
            def _():
                signal(barrier, device)

    pl.semaphore_wait(barrier, count)

    def p_copy(k):
        return remote(
            partial, parts.at[col], psend.at[k - 1], precv.at[k - 1], (row, lax.rem(col + k, n_col))
        )

    def q_copy(k):
        return remote(
            spread.at[row], spread.at[row], qsend.at[k - 1], qrecv.at[k - 1],
            (lax.rem(row + k, n_row), col),
        )

    def near_copy(dr, dc):
        device = near[dr, dc][1]
        vertical = pl.ds(height - EDGE, EDGE) if dr == 1 else pl.ds(0, EDGE)
        k = (dr + 1) * 3 + dc + 1
        v = 0 if dr == 1 else 1
        if dc == 0:
            src, dst = diff.at[:, vertical, :], rows_out.at[v]
        elif dr == 0:
            src = edges.at[:, pl.ds(EDGE if dc == 1 else 0, EDGE), :]
            dst = sides.at[0 if dc == 1 else 1]
        else:
            lanes = pl.ds(length - LANES, LANES) if dc == 1 else pl.ds(0, LANES)
            src = diff.at[:, vertical, lanes]
            dst = corners.at[v * 2 + (0 if dc == 1 else 1)]
        return remote(src, dst, nsend.at[k], nrecv.at[k], device)

    for k in range(1, n_col):
        p_copy(k).start()
    for (dr, dc), (exists, _) in near.items():
        pl.when(exists)(near_copy(dr, dc).start)
    own = [
        jnp.dot(partial[s], hc[0, col], precision=HIGHEST, preferred_element_type=F32)
        for s in range(scans)
    ]
    for k in range(1, n_col):
        p_copy(k).wait_recv()
        source = lax.rem(col - k + n_col, n_col)
        for s in range(scans):
            own[s] = own[s] + jnp.dot(
                parts[source, s], hc[0, source], precision=HIGHEST, preferred_element_type=F32
            )
    for s in range(scans):
        spread[row, s] = own[s]
    for k in range(1, n_row):
        q_copy(k).start()
    for k in range(1, n_col):
        p_copy(k).wait_send()
    for (dr, dc), (exists, _) in near.items():
        pl.when(exists)(near_copy(dr, dc).wait_send)
        pl.when(near[-dr, -dc][0])(near_copy(dr, dc).wait_recv)
    for k in range(1, n_row):
        q_copy(k).wait_send()
        q_copy(k).wait_recv()


def band_kernel(n_row, n_col, place, diff, rows_in, corners, sides, spread, ru, cu, rw, cw,
                band_out, slope_out, sums, x, a, b):
    row, col = place[0], place[1]
    height, length = diff.shape[1], diff.shape[2]
    width = length + 2 * LANES
    tall = height + 2 * EDGE
    zero = jnp.float32(0.0)
    has_top, has_bottom = row > 0, row < n_row - 1
    has_left, has_right = col > 0, col < n_col - 1
    mid = slice(LANES, LANES + length)
    x[EDGE : EDGE + height, mid] = diff[0]
    x[0:EDGE, mid] = jnp.where(has_top, rows_in[0, 0], zero)
    x[EDGE + height :, mid] = jnp.where(has_bottom, rows_in[1, 0], zero)
    x[0:EDGE, 0:LANES] = jnp.where(has_top & has_left, corners[0, 0], zero)
    x[0:EDGE, LANES + length :] = jnp.where(has_top & has_right, corners[1, 0], zero)
    x[EDGE + height :, 0:LANES] = jnp.where(has_bottom & has_left, corners[2, 0], zero)
    x[EDGE + height :, LANES + length :] = jnp.where(has_bottom & has_right, corners[3, 0], zero)
    blank = jnp.zeros((LANES - EDGE, height), F32)
    left = jnp.where(has_left, sides[0, 0], zero)
    right = jnp.where(has_right, sides[1, 0], zero)
    x[EDGE : EDGE + height, 0:LANES] = jnp.transpose(jnp.concatenate([blank, left], axis=0))
    x[EDGE : EDGE + height, LANES + length :] = jnp.transpose(
        jnp.concatenate([right, blank], axis=0)
    )

    def across(r, carry):
        here = pl.ds(pl.multiple_of(r * 16, 16), 16)
        v = x[here, :]
        total = TAPS[SR] * v
        for k in range(1, SR + 1):
            total = total + TAPS[SR + k] * (pltpu.roll(v, k, 1) + pltpu.roll(v, width - k, 1))
        a[here, :] = total * cw[0]
        return carry

    lax.fori_loop(0, tall // 16, across, 0)
    q = jnp.concatenate([spread[i, 0] for i in range(n_row)], axis=0)
    mixed = jnp.dot(ru[0], q, precision=HIGHEST, preferred_element_type=F32)
    pieces = jnp.concatenate(split3(mixed), axis=1)
    cub = cu[0].astype(BF16)
    wavy = jnp.dot(pieces, jnp.concatenate([cub, cub, cub], axis=0), preferred_element_type=F32)
    b[...] = wavy

    def along(r, carry):
        base = pl.multiple_of(r * 8, 8)
        v = a[pl.ds(base, 24), :]
        total = TAPS[SR] * v[8:16]
        for k in range(1, SR + 1):
            total = total + TAPS[SR + k] * (v[8 - k : 16 - k] + v[8 + k : 16 + k])
        here = pl.ds(base + 8, 8)
        b[here, :] = total * rw[0, here, :] - b[here, :]
        return carry

    lax.fori_loop(0, height // 8, along, 0)
    for edge in (EDGE - 1, EDGE + height):
        total = TAPS[SR] * a[edge : edge + 1, :]
        for k in range(1, SR + 1):
            total = total + TAPS[SR + k] * (
                a[edge - k : edge - k + 1, :] + a[edge + k : edge + k + 1, :]
            )
        b[edge : edge + 1, :] = total * rw[0, edge : edge + 1, :] - b[edge : edge + 1, :]

    lane = lax.broadcasted_iota(jnp.int32, (1, length), 1) + col * length
    col_mask = ((lane >= 1) & (lane <= n_col * length - 2)).astype(F32)

    def slope(r, carry):
        base = pl.multiple_of(r * 8, 8)
        v = b[pl.ds(base, 24), :]
        center = v[8:16]
        gc = (pltpu.roll(center, width - 1, 1) - pltpu.roll(center, 1, 1))[:, mid] * col_mask
        index = lax.broadcasted_iota(jnp.int32, (8, 1), 0) + row * height + base
        row_mask = ((index >= 1) & (index <= n_row * height - 2)).astype(F32)
        gr = (v[9:17, mid] - v[7:15, mid]) * row_mask
        value = gc * gc + gr * gr
        field = center[:, mid]
        here = pl.ds(base, 8)
        band_out[0, here, :] = field
        slope_out[0, here, :] = value
        return carry[0] + field * field, carry[1] + value

    start = jnp.zeros((8, length), F32)
    heights, slopes = lax.fori_loop(0, height // 8, slope, (start, start))
    sums[0, 0] = sum(heights[:, i : i + LANES] for i in range(0, length, LANES))
    sums[0, 1] = sum(slopes[:, i : i + LANES] for i in range(0, length, LANES))


def body(n_row, n_col, before, after, offsets, fractions):
    scans, height, length = before.shape
    width = length + 2 * LANES
    tall = height + 2 * EDGE
    r_tab, c_tab, hc, cu, ru, rw, cw = tables(n_row * height, n_col * length, height, length)
    pr = r_tab.shape[1]
    place = jnp.stack([lax.axis_index("row"), lax.axis_index("col")]).astype(jnp.int32)
    filler = jnp.zeros((scans, height, 5), F32)
    extra = jnp.concatenate(
        [after[:, :, LANES : LANES + 2], filler, after[:, :, length - LANES - 1 : length - LANES]], axis=2
    ).transpose(0, 2, 1)
    struct = jax.ShapeDtypeStruct
    dma = pltpu.SemaphoreType.DMA
    wide, slots = pl.pallas_call(
        functools.partial(halo_kernel, n_row, n_col),
        out_shape=(
            struct((scans, height + 2 * HALO, width), F32),
            struct((6, scans, 8, height), F32),
        ),
        in_specs=[ANY, ANY],
        out_specs=(ANY, ANY),
        scratch_shapes=[dma, dma((8, scans)), dma((8, scans)), dma((6,)), dma((6,))],
        compiler_params=pltpu.CompilerParams(
            collective_id=0, has_side_effects=True, vmem_limit_bytes=VMEM_LIMIT
        ),
        name="halo",
    )(after, extra)

    by_scan = lambda s, *_: (s, 0, 0)
    row_part = lambda s, p, *_: (p[0], 0, 0)
    col_part = lambda s, p, *_: (p[1], 0, 0)
    diff, partial, edges = pl.pallas_call(
        shift_kernel,
        out_shape=(
            struct((scans, height, length), F32),
            struct((scans, pr, LANES), F32),
            struct((scans, 2 * EDGE, height), F32),
        ),
        grid_spec=pltpu.PrefetchScalarGridSpec(
            num_scalar_prefetch=3,
            grid=(scans,),
            in_specs=[
                pl.BlockSpec((1, height + 2 * HALO, width), by_scan),
                pl.BlockSpec((1, height, length), by_scan),
                pl.BlockSpec((6, 1, 8, height), lambda s, *_: (0, s, 0, 0)),
                pl.BlockSpec((1, pr, height), row_part),
                pl.BlockSpec((1, length, LANES), col_part),
            ],
            out_specs=(
                pl.BlockSpec((1, height, length), by_scan),
                pl.BlockSpec((1, pr, LANES), by_scan),
                pl.BlockSpec((1, 2 * EDGE, height), by_scan),
            ),
            scratch_shapes=[pltpu.VMEM((height + 2 * HALO, LANES), F32)],
        ),
        compiler_params=pltpu.CompilerParams(vmem_limit_bytes=VMEM_LIMIT),
        name="shift",
    )(place, offsets[:, :, 0, 0], fractions[:, :, 0, 0], wide, before, slots, r_tab, c_tab)

    hc_here = lax.dynamic_index_in_dim(jnp.asarray(hc), place[1], 0, keepdims=True)
    rows_out, corners, sides, spread = pl.pallas_call(
        functools.partial(gather_kernel, n_row, n_col),
        out_shape=(
            struct((2, scans, EDGE, length), F32),
            struct((4, scans, EDGE, LANES), F32),
            struct((2, scans, EDGE, height), F32),
            struct((n_row, scans, pr, LANES), F32),
        ),
        in_specs=[ANY, VM, VM, VM],
        out_specs=(VM, VM, VM, VM),
        scratch_shapes=[
            pltpu.VMEM((n_col, scans, pr, LANES), F32),
            dma((n_col - 1,)), dma((n_col - 1,)), dma((n_row - 1,)), dma((n_row - 1,)),
            dma((9,)), dma((9,)),
        ],
        compiler_params=pltpu.CompilerParams(
            collective_id=1, has_side_effects=True, vmem_limit_bytes=VMEM_LIMIT
        ),
        name="gather",
    )(diff, partial, edges, hc_here)

    all_scan = lambda s, *_: (0, s, 0, 0)
    band, slope, sums = pl.pallas_call(
        functools.partial(band_kernel, n_row, n_col),
        out_shape=(
            struct((scans, height, length), F32),
            struct((scans, height, length), F32),
            struct((scans, 2, 8, LANES), F32),
        ),
        grid_spec=pltpu.PrefetchScalarGridSpec(
            num_scalar_prefetch=1,
            grid=(scans,),
            in_specs=[
                pl.BlockSpec((1, height, length), by_scan),
                pl.BlockSpec((2, 1, EDGE, length), all_scan),
                pl.BlockSpec((4, 1, EDGE, LANES), all_scan),
                pl.BlockSpec((2, 1, EDGE, height), all_scan),
                pl.BlockSpec((n_row, 1, pr, LANES), all_scan),
                pl.BlockSpec((1, tall, n_row * pr), row_part),
                pl.BlockSpec((1, LANES, width), col_part),
                pl.BlockSpec((1, tall, 1), row_part),
                pl.BlockSpec((1, 1, width), col_part),
            ],
            out_specs=(
                pl.BlockSpec((1, height, length), by_scan),
                pl.BlockSpec((1, height, length), by_scan),
                pl.BlockSpec((1, 2, 8, LANES), lambda s, *_: (s, 0, 0, 0)),
            ),
            scratch_shapes=[pltpu.VMEM((tall, width), F32)] * 3,
        ),
        compiler_params=pltpu.CompilerParams(vmem_limit_bytes=VMEM_LIMIT),
        name="band",
    )(place, diff, rows_out, corners, sides, spread, ru, cu, rw, cw)
    totals = lax.psum(jnp.sum(sums, axis=(2, 3)).T, ("row", "col"))
    cells = n_row * height * n_col * length
    return band, slope, jnp.sqrt(totals / cells + EPSILON)


def solution(mesh):
    n_row, n_col = mesh.shape["row"], mesh.shape["col"]
    spec = P(None, "row", "col")
    small = P(None, None, "row", "col")
    return jax.shard_map(
        functools.partial(body, n_row, n_col),
        mesh=mesh,
        in_specs=(spec, spec, small, small),
        out_specs=(spec, spec, P()),
        check_vma=False,
    )
```

```python
import functools
import math

import jax
import jax.numpy as jnp
import ml_dtypes
import numpy as np
from jax import lax
from jax.experimental import pallas as pl
from jax.experimental.pallas import tpu as pltpu
from jax.sharding import PartitionSpec as P

LS = 5
SR = 4
LCUT = 1600
BLOCK = 16
DRIFT = 128
EPSILON = 1e-06
ALPHA = math.sqrt(math.log(2.0) / math.pi)
TAPS = [math.exp(-math.pi * (k / (ALPHA * LS)) ** 2) for k in range(-SR, SR + 1)]
HALO = 136
LANES = 128
EDGE = 8
F32 = jnp.float32
BF16 = jnp.bfloat16
HIGHEST = lax.Precision.HIGHEST
MESH = pl.DeviceIdType.MESH
ANY = pl.BlockSpec(memory_space=pl.ANY)
VM = pl.BlockSpec(memory_space=pltpu.VMEM)
VMEM_LIMIT = 56 * 1024 * 1024


def short_matrix(count):
    index = np.arange(count)
    matrix = np.zeros((count, count), np.float64)
    for k in range(-SR, SR + 1):
        rows = index[(index + k >= 0) & (index + k < count)]
        matrix[rows, rows + k] = TAPS[k + SR]
    return matrix, matrix.sum(axis=1)


def coarse_table(count, tile, padded):
    parts = count // tile
    blocks = tile // BLOCK
    _, weight = short_matrix(count)
    table = np.zeros((parts, padded, tile), np.float64)
    for part in range(parts):
        for b in range(-1, blocks + 1):
            target = part * blocks + b
            if target < 0 or target >= count // BLOCK:
                continue
            for p in range(target * BLOCK, (target + 1) * BLOCK):
                for k in range(-SR, SR + 1):
                    source = p + k - part * tile
                    if 0 <= source < tile:
                        table[part, b + 1, source] += TAPS[k + SR] / weight[p] / BLOCK
    return table


def long_matrix(blocks):
    index = np.arange(blocks)
    distance = (index[:, None] - index[None, :]) * BLOCK / (ALPHA * LCUT)
    matrix = np.exp(-math.pi * distance * distance)
    return matrix / matrix.sum(axis=1, keepdims=True)


def upsample_rows(count, first, length):
    blocks = count // BLOCK
    result = np.zeros((length, blocks), np.float64)
    for n in range(length):
        p = first + n
        if p < 0 or p >= count:
            continue
        u = (2 * p + 1 - BLOCK) / (2 * BLOCK)
        i = math.floor(u)
        f = u - i
        if i < 0:
            i, f = 0, 0.0
        if i >= blocks - 1:
            i, f = blocks - 1, 0.0
        result[n, i] += 1 - f
        if f:
            result[n, i + 1] += f
    return result


def spread_table(count, tile, padded):
    parts, blocks = count // tile, tile // BLOCK
    total = count // BLOCK
    table = np.zeros((total, parts, padded), np.float64)
    matrix = long_matrix(total)
    for part in range(parts):
        for b in range(-1, blocks + 1):
            source = part * blocks + b
            if 0 <= source < total:
                table[:, part, b + 1] = matrix[:, source]
    return table


def halves(table):
    high = table.astype(ml_dtypes.bfloat16)
    low = (table - high.astype(np.float64)).astype(ml_dtypes.bfloat16)
    return np.concatenate([high, low], axis=1)


@functools.lru_cache(maxsize=None)
def tables(nr, nc, tr, tc):
    n_row, n_col = nr // tr, nc // tc
    br, bc = tr // BLOCK, tc // BLOCK
    pr = -(-(br + 2) // 8) * 8
    r_table = coarse_table(nr, tr, pr)
    c_table = coarse_table(nc, tc, LANES).transpose(0, 2, 1)
    col_spread = spread_table(nc, tc, LANES)
    hc = np.zeros((n_col, n_col, LANES, LANES))
    cu = np.zeros((n_col, LANES, tc + 2 * LANES))
    for part in range(n_col):
        for b in range(-1, bc + 1):
            target = part * bc + b
            if 0 <= target < nc // BLOCK:
                hc[:, part, :, b + 1] = col_spread[target]
        up = upsample_rows(nc, part * tc - LANES, tc + 2 * LANES)
        for b in range(-1, bc + 1):
            target = part * bc + b
            if 0 <= target < nc // BLOCK:
                cu[part, b + 1] = up[:, target]
    row_spread = spread_table(nr, tr, pr).reshape(nr // BLOCK, n_row * pr)
    ru = np.stack(
        [upsample_rows(nr, part * tr - EDGE, tr + 2 * EDGE) @ row_spread for part in range(n_row)]
    )
    _, row_weight = short_matrix(nr)
    _, col_weight = short_matrix(nc)
    rw = np.zeros((n_row, tr + 2 * EDGE, 1))
    cw = np.zeros((n_col, 1, tc + 2 * LANES))
    for part in range(n_row):
        for n in range(tr + 2 * EDGE):
            p = part * tr - EDGE + n
            if 0 <= p < nr:
                rw[part, n, 0] = 1.0 / row_weight[p]
    for part in range(n_col):
        for n in range(tc + 2 * LANES):
            q = part * tc - LANES + n
            if 0 <= q < nc:
                cw[part, 0, n] = 1.0 / col_weight[q]
    gc = np.zeros((4 * LANES, 2 * LANES))
    for n in range(2 * LANES):
        for k in range(-SR, SR + 1):
            gc[n + LANES + k, n] = TAPS[k + SR]
    tall = tr + 2 * EDGE
    gr = np.zeros((n_row, tall, tall))
    for part in range(n_row):
        for n in range(SR, tall - SR):
            for k in range(-SR, SR + 1):
                gr[part, n, n + k] = TAPS[k + SR] * rw[part, n, 0]
    wide = [t.astype(np.float32) for t in (c_table, hc, cu, ru, cw)]
    return wide + [halves(t) for t in (r_table, gc[None], gr)]


def remote(src, dst, send, recv, device):
    return pltpu.make_async_remote_copy(
        src_ref=src, dst_ref=dst, send_sem=send, recv_sem=recv,
        device_id=device, device_id_type=MESH,
    )


def signal(barrier, device):
    pl.semaphore_signal(barrier, inc=1, device_id=device, device_id_type=MESH)


def neighbours(n_row, n_col):
    row, col = lax.axis_index("row"), lax.axis_index("col")
    found = {}
    for dr in (-1, 0, 1):
        for dc in (-1, 0, 1):
            if dr == 0 and dc == 0:
                continue
            r, c = row + dr, col + dc
            exists = (r >= 0) & (r < n_row) & (c >= 0) & (c < n_col)
            found[dr, dc] = (exists, (r, c))
    return found


def halo_kernel(n_row, n_col, after, extra, ends, flanks, slots, send, recv, slot_send, slot_recv):
    scans, height, length = after.shape
    near = neighbours(n_row, n_col)
    barrier = pltpu.get_barrier_semaphore()
    count = jnp.int32(0)
    for exists, device in near.values():
        count += exists.astype(jnp.int32)

        @pl.when(exists)
        def _():
            signal(barrier, device)

    pl.semaphore_wait(barrier, count)

    def row_copy(s, dr):
        src = pl.ds(height - HALO, HALO) if dr == 1 else pl.ds(0, HALO)
        k = 0 if dr == 1 else 1
        return remote(
            after.at[s, src, :], ends.at[k, s, :, pl.ds(LANES, length)],
            send.at[k, s], recv.at[k, s], near[dr, 0][1],
        )

    def col_copy(s, dc, band):
        side = 0 if dc == 1 else 1
        k = 2 + (band + 1) * 2 + side
        first = length - LANES if dc == 1 else 0
        if band == 0:
            src, dst = after.at[s, :, pl.ds(first, LANES)], flanks.at[side, s]
        else:
            v = 0 if band == -1 else 1
            src = ends.at[v, s, :, pl.ds(LANES + first, LANES)]
            dst = ends.at[v, s, :, pl.ds(0 if dc == 1 else LANES + length, LANES)]
        return remote(src, dst, send.at[k, s], recv.at[k, s], near[0, dc][1])

    def slot_copy(dr, dc):
        k = (0 if dc == 1 else 3) + (1 - dr)
        return remote(extra, slots.at[k], slot_send.at[k], slot_recv.at[k], near[dr, dc][1])

    def when(pred, action):
        pl.when(pred)(action)

    for s in range(scans):
        for dr in (1, -1):
            when(near[dr, 0][0], row_copy(s, dr).start)
    for s in range(scans):
        for dc in (1, -1):
            when(near[0, dc][0], col_copy(s, dc, 0).start)
    for dc in (1, -1):
        for dr in (-1, 0, 1):
            when(near[dr, dc][0], slot_copy(dr, dc).start)
    for s in range(scans):
        for dr in (1, -1):
            source = near[-dr, 0][0]
            when(source, row_copy(s, dr).wait_recv)
            for dc in (1, -1):
                when(source & near[0, dc][0], col_copy(s, dc, -dr).start)
    for s in range(scans):
        for dr in (1, -1):
            when(near[dr, 0][0], row_copy(s, dr).wait_send)
        for dc in (1, -1):
            for band in (-1, 0, 1):
                ok = jnp.bool_(True) if band == 0 else near[band, 0][0]
                when(ok & near[0, dc][0], col_copy(s, dc, band).wait_send)
                when(ok & near[0, -dc][0], col_copy(s, dc, band).wait_recv)
    for dc in (1, -1):
        for dr in (-1, 0, 1):
            when(near[dr, dc][0], slot_copy(dr, dc).wait_send)
            when(near[-dr, -dc][0], slot_copy(dr, dc).wait_recv)


def split2(value):
    high = value.astype(BF16)
    return high, (value - high.astype(F32)).astype(BF16)


def split3(value):
    a = value.astype(BF16)
    rest = value - a.astype(F32)
    b = rest.astype(BF16)
    c = (rest - b.astype(F32)).astype(BF16)
    return a, b, c


def cubic(t):
    t2 = t * t
    t3 = t2 * t
    return (
        0.5 * (2.0 * t2 - t3 - t),
        0.5 * (3.0 * t3 - 5.0 * t2 + 2.0),
        0.5 * (4.0 * t2 - 3.0 * t3 + t),
        0.5 * (t3 - t2),
    )


def shift_kernel(place, offsets, fractions, after, ends, flanks, before, slots, r_tab, c_tab, h_tab,
                 diff, partial, edges, wide):
    s = pl.program_id(0)
    height, length = before.shape[1], before.shape[2]
    total = length + 3 * LANES
    dr, dc = offsets[0, s], offsets[1, s]
    rt = cubic(fractions[0, s].astype(F32) / 256.0)
    ct = cubic(fractions[1, s].astype(F32) / 256.0)
    blank = jnp.zeros((LANES - 16, height), F32)
    spare = slice(length + 2 * LANES, total)
    for j in range(3):
        block = jnp.concatenate([slots[3 + j, 0], blank, slots[j, 0]], axis=0)
        flipped = jnp.transpose(block)
        if j == 0:
            wide[0:HALO, spare] = flipped[height - HALO :]
        elif j == 1:
            wide[HALO : HALO + height, spare] = flipped
        else:
            wide[HALO + height :, spare] = flipped[:HALO]
    wide[0:HALO, 0 : length + 2 * LANES] = ends[0, 0]
    wide[HALO : HALO + height, 0:LANES] = flanks[0, 0]
    wide[HALO : HALO + height, LANES : LANES + length] = after[0]
    wide[HALO : HALO + height, LANES + length : length + 2 * LANES] = flanks[1, 0]
    wide[HALO + height :, 0 : length + 2 * LANES] = ends[1, 0]
    turn = 2 * total - LANES - dc + 1
    turn = lax.rem(turn, total)
    start = HALO - 1 + dr
    rows = 32

    def step(r, carry):
        first = start + r * rows
        base = pl.multiple_of((first // 8) * 8, 8)
        off = first - base
        x = wide[pl.ds(base, rows + 16), :]
        x = pltpu.roll(x, lax.rem(rows + 16 - off, rows + 16), 0)
        y = rt[0] * x[0:rows] + rt[1] * x[1 : rows + 1] + rt[2] * x[2 : rows + 2] + rt[3] * x[3 : rows + 3]
        y = pltpu.roll(y, turn, 1)
        z = ct[0] * y[:, 0:length]
        for b in range(1, 4):
            z = z + ct[b] * pltpu.roll(y, total - b, 1)[:, 0:length]
        here = pl.ds(pl.multiple_of(r * rows, rows), rows)
        diff[0, here, :] = before[0, here, :] - z
        return carry

    lax.fori_loop(0, height // rows, step, 0)
    high, low = split2(diff[0])
    rr = r_tab[0]
    pr = rr.shape[0] // 2
    both = jnp.dot(rr, high, preferred_element_type=F32)
    mixed = both[:pr] + both[pr:] + jnp.dot(rr[:pr], low, preferred_element_type=F32)
    here = jnp.dot(mixed, c_tab[0], precision=HIGHEST, preferred_element_type=F32)
    for t in range(partial.shape[0]):
        partial[t, 0] = jnp.dot(here, h_tab[0, t], precision=HIGHEST, preferred_element_type=F32)
    edges[0, 0:EDGE] = jnp.transpose(diff[0, :, 0:LANES])[0:EDGE]
    edges[0, EDGE:] = jnp.transpose(diff[0, :, length - LANES :])[LANES - EDGE :]


def gather_kernel(n_row, n_col, diff, partial, edges, rows_out, corners, sides, spread, parts,
                  psend, precv, qsend, qrecv, nsend, nrecv):
    scans, height, length = diff.shape
    near = neighbours(n_row, n_col)
    row, col = lax.axis_index("row"), lax.axis_index("col")
    barrier = pltpu.get_barrier_semaphore()
    count = jnp.int32(n_row - 1 + n_col - 1)
    for k in range(1, n_col):
        signal(barrier, (row, lax.rem(col + k, n_col)))
    for k in range(1, n_row):
        signal(barrier, (lax.rem(row + k, n_row), col))
    for (dr, dc), (exists, device) in near.items():
        if dr and dc:
            count += exists.astype(jnp.int32)

            @pl.when(exists)
            def _():
                signal(barrier, device)

    pl.semaphore_wait(barrier, count)

    def p_copy(k):
        target = lax.rem(col + k, n_col)
        return remote(
            partial.at[target], parts.at[col], psend.at[k - 1], precv.at[k - 1], (row, target)
        )

    def q_copy(k):
        return remote(
            spread.at[row], spread.at[row], qsend.at[k - 1], qrecv.at[k - 1],
            (lax.rem(row + k, n_row), col),
        )

    def near_copy(dr, dc):
        device = near[dr, dc][1]
        vertical = pl.ds(height - EDGE, EDGE) if dr == 1 else pl.ds(0, EDGE)
        k = (dr + 1) * 3 + dc + 1
        v = 0 if dr == 1 else 1
        if dc == 0:
            src, dst = diff.at[:, vertical, :], rows_out.at[v]
        elif dr == 0:
            src = edges.at[:, pl.ds(EDGE if dc == 1 else 0, EDGE), :]
            dst = sides.at[0 if dc == 1 else 1]
        else:
            lanes = pl.ds(length - LANES, LANES) if dc == 1 else pl.ds(0, LANES)
            src = diff.at[:, vertical, lanes]
            dst = corners.at[v * 2 + (0 if dc == 1 else 1)]
        return remote(src, dst, nsend.at[k], nrecv.at[k], device)

    for k in range(1, n_col):
        p_copy(k).start()
    for (dr, dc), (exists, _) in near.items():
        pl.when(exists)(near_copy(dr, dc).start)
    own = partial[col]
    for k in range(1, n_col):
        p_copy(k).wait_recv()
        own = own + parts[lax.rem(col - k + n_col, n_col)]
    spread[row] = own
    for k in range(1, n_row):
        q_copy(k).start()
    for k in range(1, n_col):
        p_copy(k).wait_send()
    for (dr, dc), (exists, _) in near.items():
        pl.when(exists)(near_copy(dr, dc).wait_send)
        pl.when(near[-dr, -dc][0])(near_copy(dr, dc).wait_recv)
    for k in range(1, n_row):
        q_copy(k).wait_send()
        q_copy(k).wait_recv()


def band_kernel(n_row, n_col, place, diff, rows_in, corners, sides, spread, ru, cu, cw, gc, gr,
                band_out, slope_out, sums, x, b):
    row, col = place[0], place[1]
    height, length = diff.shape[1], diff.shape[2]
    width = length + 2 * LANES
    tall = height + 2 * EDGE
    zero = jnp.float32(0.0)
    has_top, has_bottom = row > 0, row < n_row - 1
    has_left, has_right = col > 0, col < n_col - 1
    mid = slice(LANES, LANES + length)
    x[EDGE : EDGE + height, mid] = diff[0]
    x[0:EDGE, mid] = jnp.where(has_top, rows_in[0, 0], zero)
    x[EDGE + height :, mid] = jnp.where(has_bottom, rows_in[1, 0], zero)
    x[0:EDGE, 0:LANES] = jnp.where(has_top & has_left, corners[0, 0], zero)
    x[0:EDGE, LANES + length :] = jnp.where(has_top & has_right, corners[1, 0], zero)
    x[EDGE + height :, 0:LANES] = jnp.where(has_bottom & has_left, corners[2, 0], zero)
    x[EDGE + height :, LANES + length :] = jnp.where(has_bottom & has_right, corners[3, 0], zero)
    blank = jnp.zeros((LANES - EDGE, height), F32)
    left = jnp.where(has_left, sides[0, 0], zero)
    right = jnp.where(has_right, sides[1, 0], zero)
    x[EDGE : EDGE + height, 0:LANES] = jnp.transpose(jnp.concatenate([blank, left], axis=0))
    x[EDGE : EDGE + height, LANES + length :] = jnp.transpose(
        jnp.concatenate([right, blank], axis=0)
    )

    high, low = split2(x[...])
    both = jnp.concatenate([high, low], axis=0)
    pieces = []
    for first in range(0, width, 2 * LANES):
        begin, end = max(first - LANES, 0), min(first + 3 * LANES, width)
        skip = begin - (first - LANES)
        g_high = gc[0, skip : skip + end - begin, :]
        g_low = gc[0, 4 * LANES + skip : 4 * LANES + skip + end - begin, :]
        two = jnp.dot(both[:, begin:end], g_high, preferred_element_type=F32)
        pieces.append(
            two[:tall] + two[tall:]
            + jnp.dot(high[:, begin:end], g_low, preferred_element_type=F32)
        )
    high, low = split2(jnp.concatenate(pieces, axis=1) * cw[0])
    two = jnp.dot(gr[0], high, preferred_element_type=F32)
    smooth = two[:tall] + two[tall:] + jnp.dot(gr[0, :tall], low, preferred_element_type=F32)
    q = jnp.concatenate([spread[i, 0] for i in range(n_row)], axis=0)
    mixed = jnp.dot(ru[0], q, precision=HIGHEST, preferred_element_type=F32)
    pieces = jnp.concatenate(split3(mixed), axis=1)
    cub = cu[0].astype(BF16)
    wavy = jnp.dot(pieces, jnp.concatenate([cub, cub, cub], axis=0), preferred_element_type=F32)
    b[...] = smooth - wavy

    lane = lax.broadcasted_iota(jnp.int32, (1, length), 1) + col * length
    col_mask = ((lane >= 1) & (lane <= n_col * length - 2)).astype(F32)

    def slope(r, carry):
        base = pl.multiple_of(r * 8, 8)
        v = b[pl.ds(base, 24), :]
        center = v[8:16]
        gc = (pltpu.roll(center, width - 1, 1) - pltpu.roll(center, 1, 1))[:, mid] * col_mask
        index = lax.broadcasted_iota(jnp.int32, (8, 1), 0) + row * height + base
        row_mask = ((index >= 1) & (index <= n_row * height - 2)).astype(F32)
        gr = (v[9:17, mid] - v[7:15, mid]) * row_mask
        value = gc * gc + gr * gr
        field = center[:, mid]
        here = pl.ds(base, 8)
        band_out[0, here, :] = field
        slope_out[0, here, :] = value
        return carry[0] + field * field, carry[1] + value

    start = jnp.zeros((8, length), F32)
    heights, slopes = lax.fori_loop(0, height // 8, slope, (start, start), unroll=2)
    sums[0, 0] = sum(heights[:, i : i + LANES] for i in range(0, length, LANES))
    sums[0, 1] = sum(slopes[:, i : i + LANES] for i in range(0, length, LANES))


def total_kernel(n_row, n_col, cells, sums, out, held, parts, psend, precv, qsend, qrecv):
    row, col = lax.axis_index("row"), lax.axis_index("col")
    scans = sums.shape[0]
    barrier = pltpu.get_barrier_semaphore()
    for k in range(1, n_col):
        signal(barrier, (row, lax.rem(col + k, n_col)))
    for k in range(1, n_row):
        signal(barrier, (lax.rem(row + k, n_row), col))
    for k in range(2):
        for s in range(scans):
            held[0, k * scans + s : k * scans + s + 1] = jnp.sum(sums[s, k], axis=0, keepdims=True)
    pl.semaphore_wait(barrier, n_row + n_col - 2)

    def p_copy(k):
        return remote(
            held.at[0], parts.at[k - 1], psend.at[k - 1], precv.at[k - 1],
            (row, lax.rem(col + k, n_col)),
        )

    def q_copy(k):
        slot = n_col - 1 + k - 1
        return remote(
            held.at[1], parts.at[slot], qsend.at[k - 1], qrecv.at[k - 1],
            (lax.rem(row + k, n_row), col),
        )

    for k in range(1, n_col):
        p_copy(k).start()
    value = held[0]
    for k in range(1, n_col):
        p_copy(k).wait_recv()
        value = value + parts[k - 1]
    held[1] = value
    for k in range(1, n_row):
        q_copy(k).start()
    for k in range(1, n_row):
        q_copy(k).wait_recv()
        value = value + parts[n_col - 1 + k - 1]
    result = jnp.sqrt(jnp.sum(value, axis=1, keepdims=True) / cells + EPSILON)
    spread = jnp.broadcast_to(result, value.shape)
    index = lax.broadcasted_iota(jnp.int32, value.shape, 0)
    lane = lax.broadcasted_iota(jnp.int32, value.shape, 1)
    for k in range(2):
        picked = jnp.sum(jnp.where(index == k * scans + lane, spread, 0.0), axis=0, keepdims=True)
        out[k : k + 1, :] = picked[:, 0:scans]
    for k in range(1, n_col):
        p_copy(k).wait_send()
    for k in range(1, n_row):
        q_copy(k).wait_send()


def body(n_row, n_col, before, after, offsets, fractions):
    scans, height, length = before.shape
    width = length + 2 * LANES
    tall = height + 2 * EDGE
    c_tab, hc, cu, ru, cw, r_tab, gc, gr = tables(n_row * height, n_col * length, height, length)
    pr = r_tab.shape[1] // 2
    place = jnp.stack([lax.axis_index("row"), lax.axis_index("col")]).astype(jnp.int32)
    filler = jnp.zeros((scans, height, 5), F32)
    extra = jnp.concatenate(
        [after[:, :, LANES : LANES + 2], filler, after[:, :, length - LANES - 1 : length - LANES]], axis=2
    ).transpose(0, 2, 1)
    struct = jax.ShapeDtypeStruct
    dma = pltpu.SemaphoreType.DMA
    ends, flanks, slots = pl.pallas_call(
        functools.partial(halo_kernel, n_row, n_col),
        out_shape=(
            struct((2, scans, HALO, width), F32),
            struct((2, scans, height, LANES), F32),
            struct((6, scans, 8, height), F32),
        ),
        in_specs=[ANY, ANY],
        out_specs=(ANY, ANY, ANY),
        scratch_shapes=[dma((8, scans)), dma((8, scans)), dma((6,)), dma((6,))],
        compiler_params=pltpu.CompilerParams(
            collective_id=0, has_side_effects=True, vmem_limit_bytes=VMEM_LIMIT
        ),
        name="halo",
    )(after, extra)

    all_scan = lambda s, *_: (0, s, 0, 0)
    by_scan = lambda s, *_: (s, 0, 0)
    row_part = lambda s, p, *_: (p[0], 0, 0)
    col_part = lambda s, p, *_: (p[1], 0, 0)
    diff, partial, edges = pl.pallas_call(
        shift_kernel,
        out_shape=(
            struct((scans, height, length), F32),
            struct((n_col, scans, pr, LANES), F32),
            struct((scans, 2 * EDGE, height), F32),
        ),
        grid_spec=pltpu.PrefetchScalarGridSpec(
            num_scalar_prefetch=3,
            grid=(scans,),
            in_specs=[
                pl.BlockSpec((1, height, length), by_scan),
                pl.BlockSpec((2, 1, HALO, width), all_scan),
                pl.BlockSpec((2, 1, height, LANES), all_scan),
                pl.BlockSpec((1, height, length), by_scan),
                pl.BlockSpec((6, 1, 8, height), lambda s, *_: (0, s, 0, 0)),
                pl.BlockSpec((1, 2 * pr, height), row_part),
                pl.BlockSpec((1, length, LANES), col_part),
                pl.BlockSpec((1, n_col, LANES, LANES), lambda s, p, *_: (p[1], 0, 0, 0)),
            ],
            out_specs=(
                pl.BlockSpec((1, height, length), by_scan),
                pl.BlockSpec((n_col, 1, pr, LANES), all_scan),
                pl.BlockSpec((1, 2 * EDGE, height), by_scan),
            ),
            scratch_shapes=[pltpu.VMEM((height + 2 * HALO, width + LANES), F32)],
        ),
        compiler_params=pltpu.CompilerParams(vmem_limit_bytes=VMEM_LIMIT),
        name="shift",
    )(place, offsets[:, :, 0, 0], fractions[:, :, 0, 0], after, ends, flanks, before, slots, r_tab, c_tab, hc)

    rows_out, corners, sides, spread = pl.pallas_call(
        functools.partial(gather_kernel, n_row, n_col),
        out_shape=(
            struct((2, scans, EDGE, length), F32),
            struct((4, scans, EDGE, LANES), F32),
            struct((2, scans, EDGE, height), F32),
            struct((n_row, scans, pr, LANES), F32),
        ),
        in_specs=[ANY, VM, VM],
        out_specs=(VM, VM, VM, VM),
        scratch_shapes=[
            pltpu.VMEM((n_col, scans, pr, LANES), F32),
            dma((n_col - 1,)), dma((n_col - 1,)), dma((n_row - 1,)), dma((n_row - 1,)),
            dma((9,)), dma((9,)),
        ],
        compiler_params=pltpu.CompilerParams(
            collective_id=1, has_side_effects=True, vmem_limit_bytes=VMEM_LIMIT
        ),
        name="gather",
    )(diff, partial, edges)

    band, slope, sums = pl.pallas_call(
        functools.partial(band_kernel, n_row, n_col),
        out_shape=(
            struct((scans, height, length), F32),
            struct((scans, height, length), F32),
            struct((scans, 2, 8, LANES), F32),
        ),
        grid_spec=pltpu.PrefetchScalarGridSpec(
            num_scalar_prefetch=1,
            grid=(scans,),
            in_specs=[
                pl.BlockSpec((1, height, length), by_scan),
                pl.BlockSpec((2, 1, EDGE, length), all_scan),
                pl.BlockSpec((4, 1, EDGE, LANES), all_scan),
                pl.BlockSpec((2, 1, EDGE, height), all_scan),
                pl.BlockSpec((n_row, 1, pr, LANES), all_scan),
                pl.BlockSpec((1, tall, n_row * pr), row_part),
                pl.BlockSpec((1, LANES, width), col_part),
                pl.BlockSpec((1, 1, width), col_part),
                pl.BlockSpec((1, 8 * LANES, 2 * LANES), lambda s, *_: (0, 0, 0)),
                pl.BlockSpec((1, 2 * tall, tall), row_part),
            ],
            out_specs=(
                pl.BlockSpec((1, height, length), by_scan),
                pl.BlockSpec((1, height, length), by_scan),
                pl.BlockSpec((1, 2, 8, LANES), lambda s, *_: (s, 0, 0, 0)),
            ),
            scratch_shapes=[pltpu.VMEM((tall, width), F32)] * 2,
        ),
        compiler_params=pltpu.CompilerParams(vmem_limit_bytes=VMEM_LIMIT),
        name="band",
    )(place, diff, rows_out, corners, sides, spread, ru, cu, cw, gc, gr)
    params = pl.pallas_call(
        functools.partial(total_kernel, n_row, n_col, float(n_row * height * n_col * length)),
        out_shape=struct((2, scans), F32),
        in_specs=[VM],
        out_specs=VM,
        scratch_shapes=[
            pltpu.VMEM((2, 2 * scans, LANES), F32),
            pltpu.VMEM((n_row + n_col - 2, 2 * scans, LANES), F32),
            dma((n_col - 1,)), dma((n_col - 1,)), dma((n_row - 1,)), dma((n_row - 1,)),
        ],
        compiler_params=pltpu.CompilerParams(collective_id=2, has_side_effects=True),
        name="total",
    )(sums)
    return band, slope, params


def solution(mesh):
    n_row, n_col = mesh.shape["row"], mesh.shape["col"]
    spec = P(None, "row", "col")
    small = P(None, None, "row", "col")
    return jax.shard_map(
        functools.partial(body, n_row, n_col),
        mesh=mesh,
        in_specs=(spec, spec, small, small),
        out_specs=(spec, spec, P()),
        check_vma=False,
    )
```

```python
import functools
import math

import jax
import jax.numpy as jnp
import ml_dtypes
import numpy as np
from jax import lax
from jax.experimental import pallas as pl
from jax.experimental.pallas import tpu as pltpu
from jax.sharding import PartitionSpec as P

LS = 5
SR = 4
LCUT = 1600
BLOCK = 16
DRIFT = 128
EPSILON = 1e-06
ALPHA = math.sqrt(math.log(2.0) / math.pi)
TAPS = [math.exp(-math.pi * (k / (ALPHA * LS)) ** 2) for k in range(-SR, SR + 1)]
HALO = 136
LANES = 128
EDGE = 8
F32 = jnp.float32
BF16 = jnp.bfloat16
HIGHEST = lax.Precision.HIGHEST
MESH = pl.DeviceIdType.MESH
ANY = pl.BlockSpec(memory_space=pl.ANY)
VM = pl.BlockSpec(memory_space=pltpu.VMEM)
VMEM_LIMIT = 56 * 1024 * 1024


def short_matrix(count):
    index = np.arange(count)
    matrix = np.zeros((count, count), np.float64)
    for k in range(-SR, SR + 1):
        rows = index[(index + k >= 0) & (index + k < count)]
        matrix[rows, rows + k] = TAPS[k + SR]
    return matrix, matrix.sum(axis=1)


def coarse_table(count, tile, padded):
    parts = count // tile
    blocks = tile // BLOCK
    _, weight = short_matrix(count)
    table = np.zeros((parts, padded, tile), np.float64)
    for part in range(parts):
        for b in range(-1, blocks + 1):
            target = part * blocks + b
            if target < 0 or target >= count // BLOCK:
                continue
            for p in range(target * BLOCK, (target + 1) * BLOCK):
                for k in range(-SR, SR + 1):
                    source = p + k - part * tile
                    if 0 <= source < tile:
                        table[part, b + 1, source] += TAPS[k + SR] / weight[p] / BLOCK
    return table


def long_matrix(blocks):
    index = np.arange(blocks)
    distance = (index[:, None] - index[None, :]) * BLOCK / (ALPHA * LCUT)
    matrix = np.exp(-math.pi * distance * distance)
    return matrix / matrix.sum(axis=1, keepdims=True)


def upsample_rows(count, first, length):
    blocks = count // BLOCK
    result = np.zeros((length, blocks), np.float64)
    for n in range(length):
        p = first + n
        if p < 0 or p >= count:
            continue
        u = (2 * p + 1 - BLOCK) / (2 * BLOCK)
        i = math.floor(u)
        f = u - i
        if i < 0:
            i, f = 0, 0.0
        if i >= blocks - 1:
            i, f = blocks - 1, 0.0
        result[n, i] += 1 - f
        if f:
            result[n, i + 1] += f
    return result


def spread_table(count, tile, padded):
    parts, blocks = count // tile, tile // BLOCK
    total = count // BLOCK
    table = np.zeros((total, parts, padded), np.float64)
    matrix = long_matrix(total)
    for part in range(parts):
        for b in range(-1, blocks + 1):
            source = part * blocks + b
            if 0 <= source < total:
                table[:, part, b + 1] = matrix[:, source]
    return table


def halves(table):
    high = table.astype(ml_dtypes.bfloat16)
    low = (table - high.astype(np.float64)).astype(ml_dtypes.bfloat16)
    return np.concatenate([high, low], axis=1)


@functools.lru_cache(maxsize=None)
def tables(nr, nc, tr, tc):
    n_row, n_col = nr // tr, nc // tc
    br, bc = tr // BLOCK, tc // BLOCK
    pr = -(-(br + 2) // 8) * 8
    r_table = coarse_table(nr, tr, pr)
    c_table = coarse_table(nc, tc, LANES).transpose(0, 2, 1)
    col_spread = spread_table(nc, tc, LANES)
    hc = np.zeros((n_col, n_col, LANES, LANES))
    cu = np.zeros((n_col, LANES, tc + 2 * LANES))
    for part in range(n_col):
        for b in range(-1, bc + 1):
            target = part * bc + b
            if 0 <= target < nc // BLOCK:
                hc[:, part, :, b + 1] = col_spread[target]
        up = upsample_rows(nc, part * tc - LANES, tc + 2 * LANES)
        for b in range(-1, bc + 1):
            target = part * bc + b
            if 0 <= target < nc // BLOCK:
                cu[part, b + 1] = up[:, target]
    row_spread = spread_table(nr, tr, pr).reshape(nr // BLOCK, n_row * pr)
    ru = np.stack(
        [upsample_rows(nr, part * tr - EDGE, tr + 2 * EDGE) @ row_spread for part in range(n_row)]
    )
    _, row_weight = short_matrix(nr)
    _, col_weight = short_matrix(nc)
    rw = np.zeros((n_row, tr + 2 * EDGE, 1))
    cw = np.zeros((n_col, 1, tc + 2 * LANES))
    for part in range(n_row):
        for n in range(tr + 2 * EDGE):
            p = part * tr - EDGE + n
            if 0 <= p < nr:
                rw[part, n, 0] = 1.0 / row_weight[p]
    for part in range(n_col):
        for n in range(tc + 2 * LANES):
            q = part * tc - LANES + n
            if 0 <= q < nc:
                cw[part, 0, n] = 1.0 / col_weight[q]
    gc = np.zeros((4 * LANES, 2 * LANES))
    for n in range(2 * LANES):
        for k in range(-SR, SR + 1):
            gc[n + LANES + k, n] = TAPS[k + SR]
    tall = tr + 2 * EDGE
    gr = np.zeros((n_row, tall, tall))
    for part in range(n_row):
        for n in range(SR, tall - SR):
            for k in range(-SR, SR + 1):
                gr[part, n, n + k] = TAPS[k + SR] * rw[part, n, 0]
    wide = [t.astype(np.float32) for t in (c_table, hc, cu, ru, cw)]
    return wide + [halves(t) for t in (r_table, gc[None], gr)]


def remote(src, dst, send, recv, device):
    return pltpu.make_async_remote_copy(
        src_ref=src, dst_ref=dst, send_sem=send, recv_sem=recv,
        device_id=device, device_id_type=MESH,
    )


def signal(barrier, device):
    pl.semaphore_signal(barrier, inc=1, device_id=device, device_id_type=MESH)


def neighbours(n_row, n_col):
    row, col = lax.axis_index("row"), lax.axis_index("col")
    found = {}
    for dr in (-1, 0, 1):
        for dc in (-1, 0, 1):
            if dr == 0 and dc == 0:
                continue
            r, c = row + dr, col + dc
            exists = (r >= 0) & (r < n_row) & (c >= 0) & (c < n_col)
            found[dr, dc] = (exists, (r, c))
    return found


def halo_kernel(n_row, n_col, after, extra, ends, flanks, slots, via, send, recv, slot_send, slot_recv,
                via_send, via_recv):
    scans, height, length = after.shape
    near = neighbours(n_row, n_col)
    barrier = pltpu.get_barrier_semaphore()
    count = jnp.int32(0)
    for exists, device in near.values():
        count += exists.astype(jnp.int32)

        @pl.when(exists)
        def _():
            signal(barrier, device)

    row, col = lax.axis_index("row"), lax.axis_index("col")
    relayed = range(scans // 2, scans) if n_row == 8 else range(0)
    routes = {1: (3, 7, 4), -1: (4, 0, 3)}
    if relayed:
        for one, others in ((0, (3, 4)), (7, (3, 4)), (3, (0, 7)), (4, (0, 7))):
            count += jnp.where(row == one, 2, 0)

            @pl.when(row == one)
            def _():
                for other in others:
                    signal(barrier, (other, col))

    pl.semaphore_wait(barrier, count)

    def row_copy(s, dr):
        src = pl.ds(height - HALO, HALO) if dr == 1 else pl.ds(0, HALO)
        k = 0 if dr == 1 else 1
        return remote(
            after.at[s, src, :], ends.at[k, s, :, pl.ds(LANES, length)],
            send.at[k, s], recv.at[k, s], near[dr, 0][1],
        )

    def first_leg(s, dr):
        src = pl.ds(height - HALO, HALO) if dr == 1 else pl.ds(0, HALO)
        k = 0 if dr == 1 else 1
        return remote(
            after.at[s, src, :], via.at[s - relayed[0]],
            send.at[k, s], via_recv.at[s - relayed[0]], (routes[dr][1], col),
        )

    def second_leg(s, dr):
        k = 0 if dr == 1 else 1
        return remote(
            via.at[s - relayed[0]], ends.at[k, s, :, pl.ds(LANES, length)],
            via_send.at[s - relayed[0]], recv.at[k, s], (routes[dr][2], col),
        )

    def col_copy(s, dc, band):
        side = 0 if dc == 1 else 1
        k = 2 + (band + 1) * 2 + side
        first = length - LANES if dc == 1 else 0
        if band == 0:
            src, dst = after.at[s, :, pl.ds(first, LANES)], flanks.at[side, s]
        else:
            v = 0 if band == -1 else 1
            src = ends.at[v, s, :, pl.ds(LANES + first, LANES)]
            dst = ends.at[v, s, :, pl.ds(0 if dc == 1 else LANES + length, LANES)]
        return remote(src, dst, send.at[k, s], recv.at[k, s], near[0, dc][1])

    def slot_copy(dr, dc):
        k = (0 if dc == 1 else 3) + (1 - dr)
        return remote(extra, slots.at[k], slot_send.at[k], slot_recv.at[k], near[dr, dc][1])

    def when(pred, action):
        pl.when(pred)(action)

    for s in relayed:
        for dr in (1, -1):
            when(row == routes[dr][0], first_leg(s, dr).start)
    for s in range(scans):
        for dr in (1, -1):
            direct = near[dr, 0][0]
            if s in relayed:
                direct = direct & (row != routes[dr][0])
            when(direct, row_copy(s, dr).start)
    for s in range(scans):
        for dc in (1, -1):
            when(near[0, dc][0], col_copy(s, dc, 0).start)
    for dc in (1, -1):
        for dr in (-1, 0, 1):
            when(near[dr, dc][0], slot_copy(dr, dc).start)
    for s in relayed:
        for dr in (1, -1):
            when(row == routes[dr][1], first_leg(s, dr).wait_recv)
            when(row == routes[dr][1], second_leg(s, dr).start)
    for s in range(scans):
        for dr in (1, -1):
            source = near[-dr, 0][0]
            when(source, row_copy(s, dr).wait_recv)
            for dc in (1, -1):
                when(source & near[0, dc][0], col_copy(s, dc, -dr).start)
    for s in range(scans):
        for dr in (1, -1):
            when(near[dr, 0][0], row_copy(s, dr).wait_send)
        for dc in (1, -1):
            for band in (-1, 0, 1):
                ok = jnp.bool_(True) if band == 0 else near[band, 0][0]
                when(ok & near[0, dc][0], col_copy(s, dc, band).wait_send)
                when(ok & near[0, -dc][0], col_copy(s, dc, band).wait_recv)
    for s in relayed:
        for dr in (1, -1):
            when(row == routes[dr][1], second_leg(s, dr).wait_send)
    for dc in (1, -1):
        for dr in (-1, 0, 1):
            when(near[dr, dc][0], slot_copy(dr, dc).wait_send)
            when(near[-dr, -dc][0], slot_copy(dr, dc).wait_recv)


def split2(value):
    high = value.astype(BF16)
    return high, (value - high.astype(F32)).astype(BF16)


def split3(value):
    a = value.astype(BF16)
    rest = value - a.astype(F32)
    b = rest.astype(BF16)
    c = (rest - b.astype(F32)).astype(BF16)
    return a, b, c


def cubic(t):
    t2 = t * t
    t3 = t2 * t
    return (
        0.5 * (2.0 * t2 - t3 - t),
        0.5 * (3.0 * t3 - 5.0 * t2 + 2.0),
        0.5 * (4.0 * t2 - 3.0 * t3 + t),
        0.5 * (t3 - t2),
    )


def shift_kernel(n_col, place, offsets, fractions, after, ends, flanks, before, slots, r_tab, c_tab,
                 h_tab, diff, partial, edges, wide, mid):
    s = pl.program_id(0)
    height, length = before.shape[1], before.shape[2]
    width = length + 2 * LANES
    dr, dc = offsets[0, s, 0, 0], offsets[1, s, 0, 0]
    rt = cubic(fractions[0, s, 0, 0].astype(F32) / 256.0)
    ct = cubic(fractions[1, s, 0, 0].astype(F32) / 256.0)
    zero = jnp.float32(0.0)
    has_left, has_right = place[1] > 0, place[1] < n_col - 1
    first, last = slice(0, LANES), slice(length + 3 * LANES, length + 4 * LANES)
    left, inner = slice(LANES, 2 * LANES), slice(2 * LANES, 2 * LANES + length)
    right = slice(2 * LANES + length, 3 * LANES + length)
    blank = jnp.zeros((LANES - 8, height), F32)
    spans = (
        (slice(0, HALO), slice(height - HALO, height)),
        (slice(HALO, HALO + height), slice(0, height)),
        (slice(HALO + height, height + 2 * HALO), slice(0, HALO)),
    )
    for j, (here, part) in enumerate(spans):
        low = jnp.transpose(jnp.concatenate([blank, slots[j, 0]], axis=0))
        high = jnp.transpose(jnp.concatenate([slots[3 + j, 0], blank], axis=0))
        wide[here, first] = jnp.where(has_left, low[part], zero)
        wide[here, last] = jnp.where(has_right, high[part], zero)
    for v in range(2):
        here = spans[2 * v][0]
        wide[here, left] = jnp.where(has_left, ends[v, 0, :, 0:LANES], zero)
        wide[here, inner] = ends[v, 0, :, LANES : LANES + length]
        wide[here, right] = jnp.where(has_right, ends[v, 0, :, LANES + length :], zero)
    here = spans[1][0]
    wide[here, left] = jnp.where(has_left, flanks[0, 0], zero)
    wide[here, inner] = after[0]
    wide[here, right] = jnp.where(has_right, flanks[1, 0], zero)
    start = HALO - 1 + dr
    lane = 2 * LANES - 1 + dc
    lane_base = pl.multiple_of((lane // LANES) * LANES, LANES)
    turn = lane - lane_base
    rows = 32

    def step(r, carry):
        top = start + r * rows
        base = pl.multiple_of((top // 8) * 8, 8)
        off = top - base
        x = wide[pl.ds(base, rows + 16), pl.ds(lane_base, width)]
        x = pltpu.roll(x, lax.rem(rows + 16 - off, rows + 16), 0)
        y = rt[0] * x[0:rows] + rt[1] * x[1 : rows + 1] + rt[2] * x[2 : rows + 2] + rt[3] * x[3 : rows + 3]
        mid[pl.ds(pl.multiple_of(r * rows, rows), rows), :] = y
        return carry

    lax.fori_loop(0, height // rows, step, 0)
    shape = (4 * LANES, 2 * LANES)
    tap = lax.broadcasted_iota(jnp.int32, shape, 0) - lax.broadcasted_iota(jnp.int32, shape, 1) - turn
    taps = jnp.zeros(shape, F32)
    for b in range(4):
        taps = jnp.where(tap == b, ct[b], taps)
    t_high, t_low = split2(taps)
    high, low = split2(mid[...])
    both = jnp.concatenate([high, low], axis=0)
    for begin in range(0, length, 2 * LANES):
        window = slice(begin, begin + 4 * LANES)
        two = jnp.dot(both[:, window], t_high, preferred_element_type=F32)
        z = two[:height] + two[height:] + jnp.dot(
            high[:, window], t_low, preferred_element_type=F32
        )
        here = slice(begin, begin + 2 * LANES)
        diff[0, :, here] = before[0, :, here] - z
    high, low = split2(diff[0])
    rr = r_tab[0]
    pr = rr.shape[0] // 2
    both = jnp.dot(rr, high, preferred_element_type=F32)
    mixed = both[:pr] + both[pr:] + jnp.dot(rr[:pr], low, preferred_element_type=F32)
    here = jnp.dot(mixed, c_tab[0], precision=HIGHEST, preferred_element_type=F32)
    for t in range(partial.shape[0]):
        partial[t, 0] = jnp.dot(here, h_tab[0, t], precision=HIGHEST, preferred_element_type=F32)
    edges[0, 0:EDGE] = jnp.transpose(diff[0, :, 0:LANES])[0:EDGE]
    edges[0, EDGE:] = jnp.transpose(diff[0, :, length - LANES :])[LANES - EDGE :]


def gather_kernel(n_row, n_col, diff, partial, edges, rows_out, corners, sides, spread, parts,
                  psend, precv, qsend, qrecv, nsend, nrecv):
    scans, height, length = diff.shape
    near = neighbours(n_row, n_col)
    row, col = lax.axis_index("row"), lax.axis_index("col")
    barrier = pltpu.get_barrier_semaphore()
    count = jnp.int32(n_row - 1 + n_col - 1)
    for k in range(1, n_col):
        signal(barrier, (row, lax.rem(col + k, n_col)))
    for k in range(1, n_row):
        signal(barrier, (lax.rem(row + k, n_row), col))
    for (dr, dc), (exists, device) in near.items():
        if dr and dc:
            count += exists.astype(jnp.int32)

            @pl.when(exists)
            def _():
                signal(barrier, device)

    pl.semaphore_wait(barrier, count)

    def p_copy(k):
        target = lax.rem(col + k, n_col)
        return remote(
            partial.at[target], parts.at[col], psend.at[k - 1], precv.at[k - 1], (row, target)
        )

    def q_copy(k):
        return remote(
            spread.at[row], spread.at[row], qsend.at[k - 1], qrecv.at[k - 1],
            (lax.rem(row + k, n_row), col),
        )

    def near_copy(dr, dc):
        device = near[dr, dc][1]
        vertical = pl.ds(height - EDGE, EDGE) if dr == 1 else pl.ds(0, EDGE)
        k = (dr + 1) * 3 + dc + 1
        v = 0 if dr == 1 else 1
        if dc == 0:
            src, dst = diff.at[:, vertical, :], rows_out.at[v]
        elif dr == 0:
            src = edges.at[:, pl.ds(EDGE if dc == 1 else 0, EDGE), :]
            dst = sides.at[0 if dc == 1 else 1]
        else:
            lanes = pl.ds(length - LANES, LANES) if dc == 1 else pl.ds(0, LANES)
            src = diff.at[:, vertical, lanes]
            dst = corners.at[v * 2 + (0 if dc == 1 else 1)]
        return remote(src, dst, nsend.at[k], nrecv.at[k], device)

    for k in range(1, n_col):
        p_copy(k).start()
    for (dr, dc), (exists, _) in near.items():
        pl.when(exists)(near_copy(dr, dc).start)
    own = partial[col]
    for k in range(1, n_col):
        p_copy(k).wait_recv()
        own = own + parts[lax.rem(col - k + n_col, n_col)]
    spread[row] = own
    for k in range(1, n_row):
        q_copy(k).start()
    for k in range(1, n_col):
        p_copy(k).wait_send()
    for (dr, dc), (exists, _) in near.items():
        pl.when(exists)(near_copy(dr, dc).wait_send)
        pl.when(near[-dr, -dc][0])(near_copy(dr, dc).wait_recv)
    for k in range(1, n_row):
        q_copy(k).wait_send()
        q_copy(k).wait_recv()


def band_kernel(n_row, n_col, place, diff, rows_in, corners, sides, spread, ru, cu, cw, gc, gr,
                band_out, slope_out, sums, x, b):
    row, col = place[0], place[1]
    height, length = diff.shape[1], diff.shape[2]
    width = length + 2 * LANES
    tall = height + 2 * EDGE
    zero = jnp.float32(0.0)
    has_top, has_bottom = row > 0, row < n_row - 1
    has_left, has_right = col > 0, col < n_col - 1
    mid = slice(LANES, LANES + length)
    x[EDGE : EDGE + height, mid] = diff[0]
    x[0:EDGE, mid] = jnp.where(has_top, rows_in[0, 0], zero)
    x[EDGE + height :, mid] = jnp.where(has_bottom, rows_in[1, 0], zero)
    x[0:EDGE, 0:LANES] = jnp.where(has_top & has_left, corners[0, 0], zero)
    x[0:EDGE, LANES + length :] = jnp.where(has_top & has_right, corners[1, 0], zero)
    x[EDGE + height :, 0:LANES] = jnp.where(has_bottom & has_left, corners[2, 0], zero)
    x[EDGE + height :, LANES + length :] = jnp.where(has_bottom & has_right, corners[3, 0], zero)
    blank = jnp.zeros((LANES - EDGE, height), F32)
    left = jnp.where(has_left, sides[0, 0], zero)
    right = jnp.where(has_right, sides[1, 0], zero)
    x[EDGE : EDGE + height, 0:LANES] = jnp.transpose(jnp.concatenate([blank, left], axis=0))
    x[EDGE : EDGE + height, LANES + length :] = jnp.transpose(
        jnp.concatenate([right, blank], axis=0)
    )

    high, low = split2(x[...])
    both = jnp.concatenate([high, low], axis=0)
    pieces = []
    for first in range(0, width, 2 * LANES):
        begin, end = max(first - LANES, 0), min(first + 3 * LANES, width)
        skip = begin - (first - LANES)
        g_high = gc[0, skip : skip + end - begin, :]
        g_low = gc[0, 4 * LANES + skip : 4 * LANES + skip + end - begin, :]
        two = jnp.dot(both[:, begin:end], g_high, preferred_element_type=F32)
        pieces.append(
            two[:tall] + two[tall:]
            + jnp.dot(high[:, begin:end], g_low, preferred_element_type=F32)
        )
    high, low = split2(jnp.concatenate(pieces, axis=1) * cw[0])
    two = jnp.dot(gr[0], high, preferred_element_type=F32)
    smooth = two[:tall] + two[tall:] + jnp.dot(gr[0, :tall], low, preferred_element_type=F32)
    q = jnp.concatenate([spread[i, 0] for i in range(n_row)], axis=0)
    mixed = jnp.dot(ru[0], q, precision=HIGHEST, preferred_element_type=F32)
    pieces = jnp.concatenate(split3(mixed), axis=1)
    cub = cu[0].astype(BF16)
    wavy = jnp.dot(pieces, jnp.concatenate([cub, cub, cub], axis=0), preferred_element_type=F32)
    b[...] = smooth - wavy

    lane = lax.broadcasted_iota(jnp.int32, (1, length), 1) + col * length
    col_mask = ((lane >= 1) & (lane <= n_col * length - 2)).astype(F32)

    def slope(r, carry):
        base = pl.multiple_of(r * 8, 8)
        v = b[pl.ds(base, 24), :]
        center = v[8:16]
        gc = (pltpu.roll(center, width - 1, 1) - pltpu.roll(center, 1, 1))[:, mid] * col_mask
        index = lax.broadcasted_iota(jnp.int32, (8, 1), 0) + row * height + base
        row_mask = ((index >= 1) & (index <= n_row * height - 2)).astype(F32)
        gr = (v[9:17, mid] - v[7:15, mid]) * row_mask
        value = gc * gc + gr * gr
        field = center[:, mid]
        here = pl.ds(base, 8)
        band_out[0, here, :] = field
        slope_out[0, here, :] = value
        return carry[0] + field * field, carry[1] + value

    start = jnp.zeros((8, length), F32)
    heights, slopes = lax.fori_loop(0, height // 8, slope, (start, start), unroll=2)
    sums[0, 0] = sum(heights[:, i : i + LANES] for i in range(0, length, LANES))
    sums[0, 1] = sum(slopes[:, i : i + LANES] for i in range(0, length, LANES))


def total_kernel(n_row, n_col, cells, sums, out, held, parts, psend, precv, qsend, qrecv):
    row, col = lax.axis_index("row"), lax.axis_index("col")
    scans = sums.shape[0]
    barrier = pltpu.get_barrier_semaphore()
    for k in range(1, n_col):
        signal(barrier, (row, lax.rem(col + k, n_col)))
    for k in range(1, n_row):
        signal(barrier, (lax.rem(row + k, n_row), col))
    for k in range(2):
        for s in range(scans):
            held[0, k * scans + s : k * scans + s + 1] = jnp.sum(sums[s, k], axis=0, keepdims=True)
    pl.semaphore_wait(barrier, n_row + n_col - 2)

    def p_copy(k):
        return remote(
            held.at[0], parts.at[k - 1], psend.at[k - 1], precv.at[k - 1],
            (row, lax.rem(col + k, n_col)),
        )

    def q_copy(k):
        slot = n_col - 1 + k - 1
        return remote(
            held.at[1], parts.at[slot], qsend.at[k - 1], qrecv.at[k - 1],
            (lax.rem(row + k, n_row), col),
        )

    for k in range(1, n_col):
        p_copy(k).start()
    value = held[0]
    for k in range(1, n_col):
        p_copy(k).wait_recv()
        value = value + parts[k - 1]
    held[1] = value
    for k in range(1, n_row):
        q_copy(k).start()
    for k in range(1, n_row):
        q_copy(k).wait_recv()
        value = value + parts[n_col - 1 + k - 1]
    result = jnp.sqrt(jnp.sum(value, axis=1, keepdims=True) / cells + EPSILON)
    spread = jnp.broadcast_to(result, value.shape)
    index = lax.broadcasted_iota(jnp.int32, value.shape, 0)
    lane = lax.broadcasted_iota(jnp.int32, value.shape, 1)
    for k in range(2):
        picked = jnp.sum(jnp.where(index == k * scans + lane, spread, 0.0), axis=0, keepdims=True)
        out[k : k + 1, :] = picked[:, 0:scans]
    for k in range(1, n_col):
        p_copy(k).wait_send()
    for k in range(1, n_row):
        q_copy(k).wait_send()


def body(n_row, n_col, before, after, offsets, fractions):
    scans, height, length = before.shape
    width = length + 2 * LANES
    tall = height + 2 * EDGE
    c_tab, hc, cu, ru, cw, r_tab, gc, gr = tables(n_row * height, n_col * length, height, length)
    pr = r_tab.shape[1] // 2
    place = jnp.stack([lax.axis_index("row"), lax.axis_index("col")]).astype(jnp.int32)
    filler = jnp.zeros((scans, height, 5), F32)
    extra = jnp.concatenate(
        [after[:, :, LANES : LANES + 2], filler, after[:, :, length - LANES - 1 : length - LANES]], axis=2
    ).transpose(0, 2, 1)
    struct = jax.ShapeDtypeStruct
    dma = pltpu.SemaphoreType.DMA
    ends, flanks, slots, _ = pl.pallas_call(
        functools.partial(halo_kernel, n_row, n_col),
        out_shape=(
            struct((2, scans, HALO, width), F32),
            struct((2, scans, height, LANES), F32),
            struct((6, scans, 8, height), F32),
            struct((scans - scans // 2, HALO, length), F32),
        ),
        in_specs=[ANY, ANY],
        out_specs=(ANY, ANY, ANY, ANY),
        scratch_shapes=[
            dma((8, scans)), dma((8, scans)), dma((6,)), dma((6,)), dma((scans,)), dma((scans,))
        ],
        compiler_params=pltpu.CompilerParams(
            collective_id=0, has_side_effects=True, vmem_limit_bytes=VMEM_LIMIT
        ),
        name="halo",
    )(after, extra)

    all_scan = lambda s, *_: (0, s, 0, 0)
    by_scan = lambda s, *_: (s, 0, 0)
    row_part = lambda s, p, *_: (p[0], 0, 0)
    col_part = lambda s, p, *_: (p[1], 0, 0)
    diff, partial, edges = pl.pallas_call(
        functools.partial(shift_kernel, n_col),
        out_shape=(
            struct((scans, height, length), F32),
            struct((n_col, scans, pr, LANES), F32),
            struct((scans, 2 * EDGE, height), F32),
        ),
        grid_spec=pltpu.PrefetchScalarGridSpec(
            num_scalar_prefetch=3,
            grid=(scans,),
            in_specs=[
                pl.BlockSpec((1, height, length), by_scan),
                pl.BlockSpec((2, 1, HALO, width), all_scan),
                pl.BlockSpec((2, 1, height, LANES), all_scan),
                pl.BlockSpec((1, height, length), by_scan),
                pl.BlockSpec((6, 1, 8, height), lambda s, *_: (0, s, 0, 0)),
                pl.BlockSpec((1, 2 * pr, height), row_part),
                pl.BlockSpec((1, length, LANES), col_part),
                pl.BlockSpec((1, n_col, LANES, LANES), lambda s, p, *_: (p[1], 0, 0, 0)),
            ],
            out_specs=(
                pl.BlockSpec((1, height, length), by_scan),
                pl.BlockSpec((n_col, 1, pr, LANES), all_scan),
                pl.BlockSpec((1, 2 * EDGE, height), by_scan),
            ),
            scratch_shapes=[
                pltpu.VMEM((height + 2 * HALO, width + 2 * LANES), F32),
                pltpu.VMEM((height, width), F32),
            ],
        ),
        compiler_params=pltpu.CompilerParams(vmem_limit_bytes=VMEM_LIMIT),
        name="shift",
    )(place, offsets, fractions, after, ends, flanks, before, slots, r_tab, c_tab, hc)

    rows_out, corners, sides, spread = pl.pallas_call(
        functools.partial(gather_kernel, n_row, n_col),
        out_shape=(
            struct((2, scans, EDGE, length), F32),
            struct((4, scans, EDGE, LANES), F32),
            struct((2, scans, EDGE, height), F32),
            struct((n_row, scans, pr, LANES), F32),
        ),
        in_specs=[ANY, VM, VM],
        out_specs=(VM, VM, VM, VM),
        scratch_shapes=[
            pltpu.VMEM((n_col, scans, pr, LANES), F32),
            dma((n_col - 1,)), dma((n_col - 1,)), dma((n_row - 1,)), dma((n_row - 1,)),
            dma((9,)), dma((9,)),
        ],
        compiler_params=pltpu.CompilerParams(
            collective_id=1, has_side_effects=True, vmem_limit_bytes=VMEM_LIMIT
        ),
        name="gather",
    )(diff, partial, edges)

    band, slope, sums = pl.pallas_call(
        functools.partial(band_kernel, n_row, n_col),
        out_shape=(
            struct((scans, height, length), F32),
            struct((scans, height, length), F32),
            struct((scans, 2, 8, LANES), F32),
        ),
        grid_spec=pltpu.PrefetchScalarGridSpec(
            num_scalar_prefetch=1,
            grid=(scans,),
            in_specs=[
                pl.BlockSpec((1, height, length), by_scan),
                pl.BlockSpec((2, 1, EDGE, length), all_scan),
                pl.BlockSpec((4, 1, EDGE, LANES), all_scan),
                pl.BlockSpec((2, 1, EDGE, height), all_scan),
                pl.BlockSpec((n_row, 1, pr, LANES), all_scan),
                pl.BlockSpec((1, tall, n_row * pr), row_part),
                pl.BlockSpec((1, LANES, width), col_part),
                pl.BlockSpec((1, 1, width), col_part),
                pl.BlockSpec((1, 8 * LANES, 2 * LANES), lambda s, *_: (0, 0, 0)),
                pl.BlockSpec((1, 2 * tall, tall), row_part),
            ],
            out_specs=(
                pl.BlockSpec((1, height, length), by_scan),
                pl.BlockSpec((1, height, length), by_scan),
                pl.BlockSpec((1, 2, 8, LANES), lambda s, *_: (s, 0, 0, 0)),
            ),
            scratch_shapes=[pltpu.VMEM((tall, width), F32)] * 2,
        ),
        compiler_params=pltpu.CompilerParams(vmem_limit_bytes=VMEM_LIMIT),
        name="band",
    )(place, diff, rows_out, corners, sides, spread, ru, cu, cw, gc, gr)
    params = pl.pallas_call(
        functools.partial(total_kernel, n_row, n_col, float(n_row * height * n_col * length)),
        out_shape=struct((2, scans), F32),
        in_specs=[VM],
        out_specs=VM,
        scratch_shapes=[
            pltpu.VMEM((2, 2 * scans, LANES), F32),
            pltpu.VMEM((n_row + n_col - 2, 2 * scans, LANES), F32),
            dma((n_col - 1,)), dma((n_col - 1,)), dma((n_row - 1,)), dma((n_row - 1,)),
        ],
        compiler_params=pltpu.CompilerParams(collective_id=2, has_side_effects=True),
        name="total",
    )(sums)
    return band, slope, params


def solution(mesh):
    n_row, n_col = mesh.shape["row"], mesh.shape["col"]
    spec = P(None, "row", "col")
    small = P(None, None, "row", "col")
    return jax.shard_map(
        functools.partial(body, n_row, n_col),
        mesh=mesh,
        in_specs=(spec, spec, small, small),
        out_specs=(spec, spec, P()),
        check_vma=False,
    )
```

```python
import functools
import math

import jax
import jax.numpy as jnp
import ml_dtypes
import numpy as np
from jax import lax
from jax.experimental import pallas as pl
from jax.experimental.pallas import tpu as pltpu
from jax.sharding import PartitionSpec as P

LS = 5
SR = 4
LCUT = 1600
BLOCK = 16
DRIFT = 128
EPSILON = 1e-06
ALPHA = math.sqrt(math.log(2.0) / math.pi)
TAPS = [math.exp(-math.pi * (k / (ALPHA * LS)) ** 2) for k in range(-SR, SR + 1)]
HALO = 136
LANES = 128
EDGE = 8
F32 = jnp.float32
BF16 = jnp.bfloat16
HIGHEST = lax.Precision.HIGHEST
MESH = pl.DeviceIdType.MESH
ANY = pl.BlockSpec(memory_space=pl.ANY)
VM = pl.BlockSpec(memory_space=pltpu.VMEM)
VMEM_LIMIT = 56 * 1024 * 1024


def short_matrix(count):
    index = np.arange(count)
    matrix = np.zeros((count, count), np.float64)
    for k in range(-SR, SR + 1):
        rows = index[(index + k >= 0) & (index + k < count)]
        matrix[rows, rows + k] = TAPS[k + SR]
    return matrix, matrix.sum(axis=1)


def coarse_table(count, tile, padded):
    parts = count // tile
    blocks = tile // BLOCK
    _, weight = short_matrix(count)
    table = np.zeros((parts, padded, tile), np.float64)
    for part in range(parts):
        for b in range(-1, blocks + 1):
            target = part * blocks + b
            if target < 0 or target >= count // BLOCK:
                continue
            for p in range(target * BLOCK, (target + 1) * BLOCK):
                for k in range(-SR, SR + 1):
                    source = p + k - part * tile
                    if 0 <= source < tile:
                        table[part, b + 1, source] += TAPS[k + SR] / weight[p] / BLOCK
    return table


def long_matrix(blocks):
    index = np.arange(blocks)
    distance = (index[:, None] - index[None, :]) * BLOCK / (ALPHA * LCUT)
    matrix = np.exp(-math.pi * distance * distance)
    return matrix / matrix.sum(axis=1, keepdims=True)


def upsample_rows(count, first, length):
    blocks = count // BLOCK
    result = np.zeros((length, blocks), np.float64)
    for n in range(length):
        p = first + n
        if p < 0 or p >= count:
            continue
        u = (2 * p + 1 - BLOCK) / (2 * BLOCK)
        i = math.floor(u)
        f = u - i
        if i < 0:
            i, f = 0, 0.0
        if i >= blocks - 1:
            i, f = blocks - 1, 0.0
        result[n, i] += 1 - f
        if f:
            result[n, i + 1] += f
    return result


def spread_table(count, tile, padded):
    parts, blocks = count // tile, tile // BLOCK
    total = count // BLOCK
    table = np.zeros((total, parts, padded), np.float64)
    matrix = long_matrix(total)
    for part in range(parts):
        for b in range(-1, blocks + 1):
            source = part * blocks + b
            if 0 <= source < total:
                table[:, part, b + 1] = matrix[:, source]
    return table


def halves(table):
    high = table.astype(ml_dtypes.bfloat16)
    low = (table - high.astype(np.float64)).astype(ml_dtypes.bfloat16)
    return np.concatenate([high, low], axis=1)


@functools.lru_cache(maxsize=None)
def tables(nr, nc, tr, tc):
    n_row, n_col = nr // tr, nc // tc
    br, bc = tr // BLOCK, tc // BLOCK
    pr = -(-(br + 2) // 8) * 8
    r_table = coarse_table(nr, tr, pr)
    c_table = coarse_table(nc, tc, LANES).transpose(0, 2, 1)
    col_spread = spread_table(nc, tc, LANES)
    hc = np.zeros((n_col, n_col, LANES, LANES))
    cu = np.zeros((n_col, LANES, tc + 2 * LANES))
    for part in range(n_col):
        for b in range(-1, bc + 1):
            target = part * bc + b
            if 0 <= target < nc // BLOCK:
                hc[:, part, :, b + 1] = col_spread[target]
        up = upsample_rows(nc, part * tc - LANES, tc + 2 * LANES)
        for b in range(-1, bc + 1):
            target = part * bc + b
            if 0 <= target < nc // BLOCK:
                cu[part, b + 1] = up[:, target]
    row_spread = spread_table(nr, tr, pr).reshape(nr // BLOCK, n_row * pr)
    ru = np.stack(
        [upsample_rows(nr, part * tr - EDGE, tr + 2 * EDGE) @ row_spread for part in range(n_row)]
    )
    _, row_weight = short_matrix(nr)
    _, col_weight = short_matrix(nc)
    rw = np.zeros((n_row, tr + 2 * EDGE, 1))
    cw = np.zeros((n_col, 1, tc + 2 * LANES))
    for part in range(n_row):
        for n in range(tr + 2 * EDGE):
            p = part * tr - EDGE + n
            if 0 <= p < nr:
                rw[part, n, 0] = 1.0 / row_weight[p]
    for part in range(n_col):
        for n in range(tc + 2 * LANES):
            q = part * tc - LANES + n
            if 0 <= q < nc:
                cw[part, 0, n] = 1.0 / col_weight[q]
    gc = np.zeros((4 * LANES, 2 * LANES))
    for n in range(2 * LANES):
        for k in range(-SR, SR + 1):
            gc[n + LANES + k, n] = TAPS[k + SR]
    tall = tr + 2 * EDGE
    gr = np.zeros((n_row, tall, tall))
    for part in range(n_row):
        for n in range(SR, tall - SR):
            for k in range(-SR, SR + 1):
                gr[part, n, n + k] = TAPS[k + SR] * rw[part, n, 0]
    wide = [t.astype(np.float32) for t in (c_table, hc, cu, ru, cw)]
    return wide + [halves(t) for t in (r_table, gc[None], gr)]


def remote(src, dst, send, recv, device):
    return pltpu.make_async_remote_copy(
        src_ref=src, dst_ref=dst, send_sem=send, recv_sem=recv,
        device_id=device, device_id_type=MESH,
    )


def signal(barrier, device):
    pl.semaphore_signal(barrier, inc=1, device_id=device, device_id_type=MESH)


def neighbours(n_row, n_col):
    row, col = lax.axis_index("row"), lax.axis_index("col")
    found = {}
    for dr in (-1, 0, 1):
        for dc in (-1, 0, 1):
            if dr == 0 and dc == 0:
                continue
            r, c = row + dr, col + dc
            exists = (r >= 0) & (r < n_row) & (c >= 0) & (c < n_col)
            found[dr, dc] = (exists, (r, c))
    return found


def shift_kernel(n_row, n_col, drift, after, before_in, extra, r_in, c_in, h_in, diff, partial, edges,
                 ends, flanks, slots, via, own, before, r_tab, c_tab, h_tab, wide, mid,
                 send, recv, slot_send, slot_recv, via_send, via_recv, load):
    scans, height, length = after.shape
    near = neighbours(n_row, n_col)
    here = (lax.axis_index("row"), lax.axis_index("col"))
    loads = [
        pltpu.make_async_copy(src, dst, load.at[k])
        for k, (src, dst) in enumerate((
            (after, own), (before_in, before), (r_in.at[here[0]], r_tab),
            (c_in.at[here[1]], c_tab), (h_in.at[here[1]], h_tab),
        ))
    ]
    for copy in loads:
        copy.start()
    barrier = pltpu.get_barrier_semaphore()
    count = jnp.int32(0)
    for exists, device in near.values():
        count += exists.astype(jnp.int32)

        @pl.when(exists)
        def _():
            signal(barrier, device)

    row, col = lax.axis_index("row"), lax.axis_index("col")
    relayed = range(scans // 2, scans) if n_row == 8 else range(0)
    routes = {1: (3, 7, 4), -1: (4, 0, 3)}
    if relayed:
        for one, others in ((0, (3, 4)), (7, (3, 4)), (3, (0, 7)), (4, (0, 7))):
            count += jnp.where(row == one, 2, 0)

            @pl.when(row == one)
            def _():
                for other in others:
                    signal(barrier, (other, col))

    pl.semaphore_wait(barrier, count)

    def row_copy(s, dr):
        src = pl.ds(height - HALO, HALO) if dr == 1 else pl.ds(0, HALO)
        k = 0 if dr == 1 else 1
        return remote(
            after.at[s, src, :], ends.at[k, s, :, pl.ds(LANES, length)],
            send.at[k, s], recv.at[k, s], near[dr, 0][1],
        )

    def first_leg(s, dr):
        src = pl.ds(height - HALO, HALO) if dr == 1 else pl.ds(0, HALO)
        k = 0 if dr == 1 else 1
        return remote(
            after.at[s, src, :], via.at[s - relayed[0]],
            send.at[k, s], via_recv.at[s - relayed[0]], (routes[dr][1], col),
        )

    def second_leg(s, dr):
        k = 0 if dr == 1 else 1
        return remote(
            via.at[s - relayed[0]], ends.at[k, s, :, pl.ds(LANES, length)],
            via_send.at[s - relayed[0]], recv.at[k, s], (routes[dr][2], col),
        )

    def col_copy(s, dc, band):
        side = 0 if dc == 1 else 1
        k = 2 + (band + 1) * 2 + side
        first = length - LANES if dc == 1 else 0
        if band == 0:
            src, dst = after.at[s, :, pl.ds(first, LANES)], flanks.at[side, s]
        else:
            v = 0 if band == -1 else 1
            src = ends.at[v, s, :, pl.ds(LANES + first, LANES)]
            dst = ends.at[v, s, :, pl.ds(0 if dc == 1 else LANES + length, LANES)]
        return remote(src, dst, send.at[k, s], recv.at[k, s], near[0, dc][1])

    def slot_copy(dr, dc):
        k = (0 if dc == 1 else 3) + (1 - dr)
        return remote(extra, slots.at[k], slot_send.at[k], slot_recv.at[k], near[dr, dc][1])

    def when(pred, action):
        pl.when(pred)(action)

    for dc in (1, -1):
        for dr in (-1, 0, 1):
            when(near[dr, dc][0], slot_copy(dr, dc).start)
    for s in relayed:
        for dr in (1, -1):
            when(row == routes[dr][0], first_leg(s, dr).start)
    for s in range(scans):
        for dr in (1, -1):
            direct = near[dr, 0][0]
            if s in relayed:
                direct = direct & (row != routes[dr][0])
            when(direct, row_copy(s, dr).start)
    for s in range(scans):
        for dc in (1, -1):
            when(near[0, dc][0], col_copy(s, dc, 0).start)
    for s in relayed:
        for dr in (1, -1):
            when(row == routes[dr][1], first_leg(s, dr).wait_recv)
            when(row == routes[dr][1], second_leg(s, dr).start)
    for copy in loads:
        copy.wait()
    for dc in (1, -1):
        for dr in (-1, 0, 1):
            when(near[-dr, -dc][0], slot_copy(dr, dc).wait_recv)

    def step(t, carry):
        @pl.when(t < scans)
        def _():
            for dr in (1, -1):
                source = near[-dr, 0][0]
                when(source, row_copy(t, dr).wait_recv)
                for dc in (1, -1):
                    when(source & near[0, dc][0], col_copy(t, dc, -dr).start)

        @pl.when(t > 0)
        def _():
            for dc in (1, -1):
                for band in (-1, 0, 1):
                    ok = jnp.bool_(True) if band == 0 else near[band, 0][0]
                    when(ok & near[0, -dc][0], col_copy(t - 1, dc, band).wait_recv)
            shift_scan(
                n_row, n_col, t - 1, drift, own, ends, flanks, before, slots, r_tab, c_tab, h_tab,
                diff, partial, edges, wide, mid,
            )

        return carry

    lax.fori_loop(0, scans + 1, step, 0)
    for s in range(scans):
        for dr in (1, -1):
            when(near[dr, 0][0], row_copy(s, dr).wait_send)
        for dc in (1, -1):
            for band in (-1, 0, 1):
                ok = jnp.bool_(True) if band == 0 else near[band, 0][0]
                when(ok & near[0, dc][0], col_copy(s, dc, band).wait_send)
    for s in relayed:
        for dr in (1, -1):
            when(row == routes[dr][1], second_leg(s, dr).wait_send)
    for dc in (1, -1):
        for dr in (-1, 0, 1):
            when(near[dr, dc][0], slot_copy(dr, dc).wait_send)


def split2(value):
    high = value.astype(BF16)
    return high, (value - high.astype(F32)).astype(BF16)


def split3(value):
    a = value.astype(BF16)
    rest = value - a.astype(F32)
    b = rest.astype(BF16)
    c = (rest - b.astype(F32)).astype(BF16)
    return a, b, c


def cubic(t):
    t2 = t * t
    t3 = t2 * t
    return (
        0.5 * (2.0 * t2 - t3 - t),
        0.5 * (3.0 * t3 - 5.0 * t2 + 2.0),
        0.5 * (4.0 * t2 - 3.0 * t3 + t),
        0.5 * (t3 - t2),
    )


def shift_scan(n_row, n_col, s, drift, after, ends, flanks, before, slots, r_tab, c_tab, h_tab,
               diff, partial, edges, wide, mid):
    scans, height, length = before.shape
    width = length + 2 * LANES
    dr, dc = drift[s], drift[scans + s]
    rt = cubic(drift[2 * scans + s].astype(F32) / 256.0)
    ct = cubic(drift[3 * scans + s].astype(F32) / 256.0)
    col = lax.axis_index("col")
    zero = jnp.float32(0.0)
    row = lax.axis_index("row")
    has_left, has_right = col > 0, col < n_col - 1
    has_rows = (row > 0, jnp.bool_(True), row < n_row - 1)
    first, last = slice(0, LANES), slice(length + 3 * LANES, length + 4 * LANES)
    left, inner = slice(LANES, 2 * LANES), slice(2 * LANES, 2 * LANES + length)
    right = slice(2 * LANES + length, 3 * LANES + length)
    blank = jnp.zeros((LANES - 8, height), F32)
    spans = (
        (slice(0, HALO), slice(height - HALO, height)),
        (slice(HALO, HALO + height), slice(0, height)),
        (slice(HALO + height, height + 2 * HALO), slice(0, HALO)),
    )
    for j, (here, part) in enumerate(spans):
        low = jnp.transpose(jnp.concatenate([blank, slots[j, s]], axis=0))
        high = jnp.transpose(jnp.concatenate([slots[3 + j, s], blank], axis=0))
        wide[here, first] = jnp.where(has_left & has_rows[j], low[part], zero)
        wide[here, last] = jnp.where(has_right & has_rows[j], high[part], zero)
    for v in range(2):
        here = spans[2 * v][0]
        found = has_rows[2 * v]
        wide[here, left] = jnp.where(has_left & found, ends[v, s, :, 0:LANES], zero)
        wide[here, inner] = jnp.where(found, ends[v, s, :, LANES : LANES + length], zero)
        wide[here, right] = jnp.where(has_right & found, ends[v, s, :, LANES + length :], zero)
    here = spans[1][0]
    wide[here, left] = jnp.where(has_left, flanks[0, s], zero)
    wide[here, inner] = after[s]
    wide[here, right] = jnp.where(has_right, flanks[1, s], zero)
    def taps_at(shape, axis, offset, weights):
        tap = lax.broadcasted_iota(jnp.int32, shape, axis)
        tap = tap - lax.broadcasted_iota(jnp.int32, shape, 1 - axis) - offset
        taps = jnp.zeros(shape, F32)
        for b in range(4):
            taps = jnp.where(tap == b, weights[b], taps)
        return split2(taps)

    t_high, t_low = taps_at((height, height + 2 * HALO), 1, HALO - 1 + dr, rt)
    high, low = split2(wide[...])
    two = jnp.dot(jnp.concatenate([t_high, t_low], axis=0), high, preferred_element_type=F32)
    mid[...] = two[:height] + two[height:] + jnp.dot(t_high, low, preferred_element_type=F32)
    t_high, t_low = taps_at((6 * LANES, 2 * LANES), 0, 2 * LANES - 1 + dc, ct)
    high, low = split2(mid[...])
    both = jnp.concatenate([high, low], axis=0)
    for begin in range(0, length, 2 * LANES):
        window = slice(begin, begin + 6 * LANES)
        two = jnp.dot(both[:, window], t_high, preferred_element_type=F32)
        z = two[:height] + two[height:] + jnp.dot(
            high[:, window], t_low, preferred_element_type=F32
        )
        here = slice(begin, begin + 2 * LANES)
        diff[s, :, here] = before[s, :, here] - z
    high, low = split2(diff[s])
    rr = r_tab[...]
    pr = rr.shape[0] // 2
    both = jnp.dot(rr, high, preferred_element_type=F32)
    mixed = both[:pr] + both[pr:] + jnp.dot(rr[:pr], low, preferred_element_type=F32)
    here = jnp.dot(mixed, c_tab[...], precision=HIGHEST, preferred_element_type=F32)
    for t in range(partial.shape[0]):
        partial[t, s] = jnp.dot(here, h_tab[t], precision=HIGHEST, preferred_element_type=F32)
    edges[s, 0:EDGE] = jnp.transpose(diff[s, :, 0:LANES])[0:EDGE]
    edges[s, EDGE:] = jnp.transpose(diff[s, :, length - LANES :])[LANES - EDGE :]


def gather_kernel(n_row, n_col, diff, partial, edges, rows_out, corners, sides, spread, parts,
                  psend, precv, qsend, qrecv, nsend, nrecv):
    scans, height, length = diff.shape
    near = neighbours(n_row, n_col)
    row, col = lax.axis_index("row"), lax.axis_index("col")
    barrier = pltpu.get_barrier_semaphore()
    count = jnp.int32(n_row - 1 + n_col - 1)
    for k in range(1, n_col):
        signal(barrier, (row, lax.rem(col + k, n_col)))
    for k in range(1, n_row):
        signal(barrier, (lax.rem(row + k, n_row), col))
    for (dr, dc), (exists, device) in near.items():
        if dr and dc:
            count += exists.astype(jnp.int32)

            @pl.when(exists)
            def _():
                signal(barrier, device)

    pl.semaphore_wait(barrier, count)

    def p_copy(k):
        target = lax.rem(col + k, n_col)
        return remote(
            partial.at[target], parts.at[col], psend.at[k - 1], precv.at[k - 1], (row, target)
        )

    def q_copy(k):
        return remote(
            spread.at[row], spread.at[row], qsend.at[k - 1], qrecv.at[k - 1],
            (lax.rem(row + k, n_row), col),
        )

    def near_copy(dr, dc):
        device = near[dr, dc][1]
        vertical = pl.ds(height - EDGE, EDGE) if dr == 1 else pl.ds(0, EDGE)
        k = (dr + 1) * 3 + dc + 1
        v = 0 if dr == 1 else 1
        if dc == 0:
            src, dst = diff.at[:, vertical, :], rows_out.at[v]
        elif dr == 0:
            src = edges.at[:, pl.ds(EDGE if dc == 1 else 0, EDGE), :]
            dst = sides.at[0 if dc == 1 else 1]
        else:
            lanes = pl.ds(length - LANES, LANES) if dc == 1 else pl.ds(0, LANES)
            src = diff.at[:, vertical, lanes]
            dst = corners.at[v * 2 + (0 if dc == 1 else 1)]
        return remote(src, dst, nsend.at[k], nrecv.at[k], device)

    for k in range(1, n_col):
        p_copy(k).start()
    for (dr, dc), (exists, _) in near.items():
        pl.when(exists)(near_copy(dr, dc).start)
    own = partial[col]
    for k in range(1, n_col):
        p_copy(k).wait_recv()
        own = own + parts[lax.rem(col - k + n_col, n_col)]
    spread[row] = own
    for k in range(1, n_row):
        q_copy(k).start()
    for k in range(1, n_col):
        p_copy(k).wait_send()
    for (dr, dc), (exists, _) in near.items():
        pl.when(exists)(near_copy(dr, dc).wait_send)
        pl.when(near[-dr, -dc][0])(near_copy(dr, dc).wait_recv)
    for k in range(1, n_row):
        q_copy(k).wait_send()
        q_copy(k).wait_recv()


def band_kernel(n_row, n_col, place, diff, rows_in, corners, sides, spread, ru, cu, cw, gc, gr,
                band_out, slope_out, sums, x, b):
    row, col = place[0], place[1]
    height, length = diff.shape[1], diff.shape[2]
    width = length + 2 * LANES
    tall = height + 2 * EDGE
    zero = jnp.float32(0.0)
    has_top, has_bottom = row > 0, row < n_row - 1
    row = lax.axis_index("row")
    has_left, has_right = col > 0, col < n_col - 1
    has_rows = (row > 0, jnp.bool_(True), row < n_row - 1)
    mid = slice(LANES, LANES + length)
    x[EDGE : EDGE + height, mid] = diff[0]
    x[0:EDGE, mid] = jnp.where(has_top, rows_in[0, 0], zero)
    x[EDGE + height :, mid] = jnp.where(has_bottom, rows_in[1, 0], zero)
    x[0:EDGE, 0:LANES] = jnp.where(has_top & has_left, corners[0, 0], zero)
    x[0:EDGE, LANES + length :] = jnp.where(has_top & has_right, corners[1, 0], zero)
    x[EDGE + height :, 0:LANES] = jnp.where(has_bottom & has_left, corners[2, 0], zero)
    x[EDGE + height :, LANES + length :] = jnp.where(has_bottom & has_right, corners[3, 0], zero)
    blank = jnp.zeros((LANES - EDGE, height), F32)
    left = jnp.where(has_left, sides[0, 0], zero)
    right = jnp.where(has_right, sides[1, 0], zero)
    x[EDGE : EDGE + height, 0:LANES] = jnp.transpose(jnp.concatenate([blank, left], axis=0))
    x[EDGE : EDGE + height, LANES + length :] = jnp.transpose(
        jnp.concatenate([right, blank], axis=0)
    )

    high, low = split2(x[...])
    both = jnp.concatenate([high, low], axis=0)
    pieces = []
    for first in range(0, width, 2 * LANES):
        begin, end = max(first - LANES, 0), min(first + 3 * LANES, width)
        skip = begin - (first - LANES)
        g_high = gc[0, skip : skip + end - begin, :]
        g_low = gc[0, 4 * LANES + skip : 4 * LANES + skip + end - begin, :]
        two = jnp.dot(both[:, begin:end], g_high, preferred_element_type=F32)
        pieces.append(
            two[:tall] + two[tall:]
            + jnp.dot(high[:, begin:end], g_low, preferred_element_type=F32)
        )
    high, low = split2(jnp.concatenate(pieces, axis=1) * cw[0])
    two = jnp.dot(gr[0], high, preferred_element_type=F32)
    smooth = two[:tall] + two[tall:] + jnp.dot(gr[0, :tall], low, preferred_element_type=F32)
    q = jnp.concatenate([spread[i, 0] for i in range(n_row)], axis=0)
    mixed = jnp.dot(ru[0], q, precision=HIGHEST, preferred_element_type=F32)
    pieces = jnp.concatenate(split3(mixed), axis=1)
    cub = cu[0].astype(BF16)
    wavy = jnp.dot(pieces, jnp.concatenate([cub, cub, cub], axis=0), preferred_element_type=F32)
    b[...] = smooth - wavy

    lane = lax.broadcasted_iota(jnp.int32, (1, length), 1) + col * length
    col_mask = ((lane >= 1) & (lane <= n_col * length - 2)).astype(F32)

    def slope(r, carry):
        base = pl.multiple_of(r * 8, 8)
        v = b[pl.ds(base, 24), :]
        center = v[8:16]
        gc = (pltpu.roll(center, width - 1, 1) - pltpu.roll(center, 1, 1))[:, mid] * col_mask
        index = lax.broadcasted_iota(jnp.int32, (8, 1), 0) + row * height + base
        row_mask = ((index >= 1) & (index <= n_row * height - 2)).astype(F32)
        gr = (v[9:17, mid] - v[7:15, mid]) * row_mask
        value = gc * gc + gr * gr
        field = center[:, mid]
        here = pl.ds(base, 8)
        band_out[0, here, :] = field
        slope_out[0, here, :] = value
        return carry[0] + field * field, carry[1] + value

    start = jnp.zeros((8, length), F32)
    heights, slopes = lax.fori_loop(0, height // 8, slope, (start, start), unroll=2)
    sums[0, 0] = sum(heights[:, i : i + LANES] for i in range(0, length, LANES))
    sums[0, 1] = sum(slopes[:, i : i + LANES] for i in range(0, length, LANES))


def total_kernel(n_row, n_col, cells, sums, out, held, parts, psend, precv, qsend, qrecv):
    row, col = lax.axis_index("row"), lax.axis_index("col")
    scans = sums.shape[0]
    barrier = pltpu.get_barrier_semaphore()
    for k in range(1, n_col):
        signal(barrier, (row, lax.rem(col + k, n_col)))
    for k in range(1, n_row):
        signal(barrier, (lax.rem(row + k, n_row), col))
    for k in range(2):
        for s in range(scans):
            held[0, k * scans + s : k * scans + s + 1] = jnp.sum(sums[s, k], axis=0, keepdims=True)
    pl.semaphore_wait(barrier, n_row + n_col - 2)

    def p_copy(k):
        return remote(
            held.at[0], parts.at[k - 1], psend.at[k - 1], precv.at[k - 1],
            (row, lax.rem(col + k, n_col)),
        )

    def q_copy(k):
        slot = n_col - 1 + k - 1
        return remote(
            held.at[1], parts.at[slot], qsend.at[k - 1], qrecv.at[k - 1],
            (lax.rem(row + k, n_row), col),
        )

    for k in range(1, n_col):
        p_copy(k).start()
    value = held[0]
    for k in range(1, n_col):
        p_copy(k).wait_recv()
        value = value + parts[k - 1]
    held[1] = value
    for k in range(1, n_row):
        q_copy(k).start()
    for k in range(1, n_row):
        q_copy(k).wait_recv()
        value = value + parts[n_col - 1 + k - 1]
    result = jnp.sqrt(jnp.sum(value, axis=1, keepdims=True) / cells + EPSILON)
    spread = jnp.broadcast_to(result, value.shape)
    index = lax.broadcasted_iota(jnp.int32, value.shape, 0)
    lane = lax.broadcasted_iota(jnp.int32, value.shape, 1)
    for k in range(2):
        picked = jnp.sum(jnp.where(index == k * scans + lane, spread, 0.0), axis=0, keepdims=True)
        out[k : k + 1, :] = picked[:, 0:scans]
    for k in range(1, n_col):
        p_copy(k).wait_send()
    for k in range(1, n_row):
        q_copy(k).wait_send()


def body(n_row, n_col, before, after, offsets, fractions):
    scans, height, length = before.shape
    width = length + 2 * LANES
    tall = height + 2 * EDGE
    c_tab, hc, cu, ru, cw, r_tab, gc, gr = tables(n_row * height, n_col * length, height, length)
    pr = r_tab.shape[1] // 2
    place = jnp.stack([lax.axis_index("row"), lax.axis_index("col")]).astype(jnp.int32)
    filler = jnp.zeros((scans, height, 5), F32)
    extra = jnp.concatenate(
        [after[:, :, LANES : LANES + 2], filler, after[:, :, length - LANES - 1 : length - LANES]], axis=2
    ).transpose(0, 2, 1)
    struct = jax.ShapeDtypeStruct
    dma = pltpu.SemaphoreType.DMA
    smem = pl.BlockSpec(memory_space=pltpu.SMEM)
    drift = jnp.concatenate([offsets.reshape(2 * scans), fractions.reshape(2 * scans)])
    diff, partial, edges = pl.pallas_call(
        functools.partial(shift_kernel, n_row, n_col),
        out_shape=(
            struct((scans, height, length), F32),
            struct((n_col, scans, pr, LANES), F32),
            struct((scans, 2 * EDGE, height), F32),
        ),
        in_specs=[smem, ANY, ANY, VM, ANY, ANY, ANY],
        out_specs=(VM, VM, VM),
        scratch_shapes=[
            pltpu.VMEM((2, scans, HALO, width), F32),
            pltpu.VMEM((2, scans, height, LANES), F32),
            pltpu.VMEM((6, scans, 8, height), F32),
            pltpu.VMEM((scans - scans // 2, HALO, length), F32),
            pltpu.VMEM((scans, height, length), F32),
            pltpu.VMEM((scans, height, length), F32),
            pltpu.VMEM(r_tab.shape[1:], BF16),
            pltpu.VMEM(c_tab.shape[1:], F32),
            pltpu.VMEM(hc.shape[1:], F32),
            pltpu.VMEM((height + 2 * HALO, width + 2 * LANES), F32),
            pltpu.VMEM((height, width + 2 * LANES), F32),
            dma((8, scans)), dma((8, scans)), dma((6,)), dma((6,)), dma((scans,)), dma((scans,)),
            dma((5,)),
        ],
        compiler_params=pltpu.CompilerParams(
            collective_id=0, has_side_effects=True, vmem_limit_bytes=VMEM_LIMIT
        ),
        name="shift",
    )(drift, after, before, extra, r_tab, c_tab, hc)

    all_scan = lambda s, *_: (0, s, 0, 0)
    by_scan = lambda s, *_: (s, 0, 0)
    row_part = lambda s, p, *_: (p[0], 0, 0)
    col_part = lambda s, p, *_: (p[1], 0, 0)
    rows_out, corners, sides, spread = pl.pallas_call(
        functools.partial(gather_kernel, n_row, n_col),
        out_shape=(
            struct((2, scans, EDGE, length), F32),
            struct((4, scans, EDGE, LANES), F32),
            struct((2, scans, EDGE, height), F32),
            struct((n_row, scans, pr, LANES), F32),
        ),
        in_specs=[ANY, VM, VM],
        out_specs=(VM, VM, VM, VM),
        scratch_shapes=[
            pltpu.VMEM((n_col, scans, pr, LANES), F32),
            dma((n_col - 1,)), dma((n_col - 1,)), dma((n_row - 1,)), dma((n_row - 1,)),
            dma((9,)), dma((9,)),
        ],
        compiler_params=pltpu.CompilerParams(
            collective_id=1, has_side_effects=True, vmem_limit_bytes=VMEM_LIMIT
        ),
        name="gather",
    )(diff, partial, edges)

    band, slope, sums = pl.pallas_call(
        functools.partial(band_kernel, n_row, n_col),
        out_shape=(
            struct((scans, height, length), F32),
            struct((scans, height, length), F32),
            struct((scans, 2, 8, LANES), F32),
        ),
        grid_spec=pltpu.PrefetchScalarGridSpec(
            num_scalar_prefetch=1,
            grid=(scans,),
            in_specs=[
                pl.BlockSpec((1, height, length), by_scan),
                pl.BlockSpec((2, 1, EDGE, length), all_scan),
                pl.BlockSpec((4, 1, EDGE, LANES), all_scan),
                pl.BlockSpec((2, 1, EDGE, height), all_scan),
                pl.BlockSpec((n_row, 1, pr, LANES), all_scan),
                pl.BlockSpec((1, tall, n_row * pr), row_part),
                pl.BlockSpec((1, LANES, width), col_part),
                pl.BlockSpec((1, 1, width), col_part),
                pl.BlockSpec((1, 8 * LANES, 2 * LANES), lambda s, *_: (0, 0, 0)),
                pl.BlockSpec((1, 2 * tall, tall), row_part),
            ],
            out_specs=(
                pl.BlockSpec((1, height, length), by_scan),
                pl.BlockSpec((1, height, length), by_scan),
                pl.BlockSpec((1, 2, 8, LANES), lambda s, *_: (s, 0, 0, 0)),
            ),
            scratch_shapes=[pltpu.VMEM((tall, width), F32)] * 2,
        ),
        compiler_params=pltpu.CompilerParams(vmem_limit_bytes=VMEM_LIMIT),
        name="band",
    )(place, diff, rows_out, corners, sides, spread, ru, cu, cw, gc, gr)
    params = pl.pallas_call(
        functools.partial(total_kernel, n_row, n_col, float(n_row * height * n_col * length)),
        out_shape=struct((2, scans), F32),
        in_specs=[VM],
        out_specs=VM,
        scratch_shapes=[
            pltpu.VMEM((2, 2 * scans, LANES), F32),
            pltpu.VMEM((n_row + n_col - 2, 2 * scans, LANES), F32),
            dma((n_col - 1,)), dma((n_col - 1,)), dma((n_row - 1,)), dma((n_row - 1,)),
        ],
        compiler_params=pltpu.CompilerParams(collective_id=2, has_side_effects=True),
        name="total",
    )(sums)
    return band, slope, params


def solution(mesh):
    n_row, n_col = mesh.shape["row"], mesh.shape["col"]
    spec = P(None, "row", "col")
    small = P(None, None, "row", "col")
    return jax.shard_map(
        functools.partial(body, n_row, n_col),
        mesh=mesh,
        in_specs=(spec, spec, small, small),
        out_specs=(spec, spec, P()),
        check_vma=False,
    )
```

```python
import functools
import math

import jax
import jax.numpy as jnp
import ml_dtypes
import numpy as np
from jax import lax
from jax.experimental import pallas as pl
from jax.experimental.pallas import tpu as pltpu
from jax.sharding import PartitionSpec as P

LS = 5
SR = 4
LCUT = 1600
BLOCK = 16
DRIFT = 128
EPSILON = 1e-06
ALPHA = math.sqrt(math.log(2.0) / math.pi)
TAPS = [math.exp(-math.pi * (k / (ALPHA * LS)) ** 2) for k in range(-SR, SR + 1)]
HALO = 136
LANES = 128
EDGE = 8
F32 = jnp.float32
BF16 = jnp.bfloat16
HIGHEST = lax.Precision.HIGHEST
MESH = pl.DeviceIdType.MESH
ANY = pl.BlockSpec(memory_space=pl.ANY)
VM = pl.BlockSpec(memory_space=pltpu.VMEM)
VMEM_LIMIT = 56 * 1024 * 1024


def short_matrix(count):
    index = np.arange(count)
    matrix = np.zeros((count, count), np.float64)
    for k in range(-SR, SR + 1):
        rows = index[(index + k >= 0) & (index + k < count)]
        matrix[rows, rows + k] = TAPS[k + SR]
    return matrix, matrix.sum(axis=1)


def coarse_table(count, tile, padded):
    parts = count // tile
    blocks = tile // BLOCK
    _, weight = short_matrix(count)
    table = np.zeros((parts, padded, tile), np.float64)
    for part in range(parts):
        for b in range(-1, blocks + 1):
            target = part * blocks + b
            if target < 0 or target >= count // BLOCK:
                continue
            for p in range(target * BLOCK, (target + 1) * BLOCK):
                for k in range(-SR, SR + 1):
                    source = p + k - part * tile
                    if 0 <= source < tile:
                        table[part, b + 1, source] += TAPS[k + SR] / weight[p] / BLOCK
    return table


def long_matrix(blocks):
    index = np.arange(blocks)
    distance = (index[:, None] - index[None, :]) * BLOCK / (ALPHA * LCUT)
    matrix = np.exp(-math.pi * distance * distance)
    return matrix / matrix.sum(axis=1, keepdims=True)


def upsample_rows(count, first, length):
    blocks = count // BLOCK
    result = np.zeros((length, blocks), np.float64)
    for n in range(length):
        p = first + n
        if p < 0 or p >= count:
            continue
        u = (2 * p + 1 - BLOCK) / (2 * BLOCK)
        i = math.floor(u)
        f = u - i
        if i < 0:
            i, f = 0, 0.0
        if i >= blocks - 1:
            i, f = blocks - 1, 0.0
        result[n, i] += 1 - f
        if f:
            result[n, i + 1] += f
    return result


def spread_table(count, tile, padded):
    parts, blocks = count // tile, tile // BLOCK
    total = count // BLOCK
    table = np.zeros((total, parts, padded), np.float64)
    matrix = long_matrix(total)
    for part in range(parts):
        for b in range(-1, blocks + 1):
            source = part * blocks + b
            if 0 <= source < total:
                table[:, part, b + 1] = matrix[:, source]
    return table


def halves(table):
    high = table.astype(ml_dtypes.bfloat16)
    low = (table - high.astype(np.float64)).astype(ml_dtypes.bfloat16)
    return np.concatenate([high, low], axis=1)


@functools.lru_cache(maxsize=None)
def tables(nr, nc, tr, tc):
    n_row, n_col = nr // tr, nc // tc
    br, bc = tr // BLOCK, tc // BLOCK
    pr = -(-(br + 2) // 8) * 8
    r_table = coarse_table(nr, tr, pr)
    c_table = coarse_table(nc, tc, LANES).transpose(0, 2, 1)
    col_spread = spread_table(nc, tc, LANES)
    hc = np.zeros((n_col, n_col, LANES, LANES))
    cu = np.zeros((n_col, LANES, tc + 2 * LANES))
    for part in range(n_col):
        for b in range(-1, bc + 1):
            target = part * bc + b
            if 0 <= target < nc // BLOCK:
                hc[:, part, :, b + 1] = col_spread[target]
        up = upsample_rows(nc, part * tc - LANES, tc + 2 * LANES)
        for b in range(-1, bc + 1):
            target = part * bc + b
            if 0 <= target < nc // BLOCK:
                cu[part, b + 1] = up[:, target]
    row_spread = spread_table(nr, tr, pr).reshape(nr // BLOCK, n_row * pr)
    ru = np.stack(
        [upsample_rows(nr, part * tr - EDGE, tr + 2 * EDGE) @ row_spread for part in range(n_row)]
    )
    _, row_weight = short_matrix(nr)
    _, col_weight = short_matrix(nc)
    rw = np.zeros((n_row, tr + 2 * EDGE, 1))
    cw = np.zeros((n_col, 1, tc + 2 * LANES))
    for part in range(n_row):
        for n in range(tr + 2 * EDGE):
            p = part * tr - EDGE + n
            if 0 <= p < nr:
                rw[part, n, 0] = 1.0 / row_weight[p]
    for part in range(n_col):
        for n in range(tc + 2 * LANES):
            q = part * tc - LANES + n
            if 0 <= q < nc:
                cw[part, 0, n] = 1.0 / col_weight[q]
    gc = np.zeros((4 * LANES, 2 * LANES))
    for n in range(2 * LANES):
        for k in range(-SR, SR + 1):
            gc[n + LANES + k, n] = TAPS[k + SR]
    tall = tr + 2 * EDGE
    gr = np.zeros((n_row, tall, tall))
    for part in range(n_row):
        for n in range(SR, tall - SR):
            for k in range(-SR, SR + 1):
                gr[part, n, n + k] = TAPS[k + SR] * rw[part, n, 0]
    wide = [t.astype(np.float32) for t in (c_table, hc, cu, ru, cw)]
    return wide + [halves(t) for t in (r_table, gc[None], gr)]


def remote(src, dst, send, recv, device):
    return pltpu.make_async_remote_copy(
        src_ref=src, dst_ref=dst, send_sem=send, recv_sem=recv,
        device_id=device, device_id_type=MESH,
    )


def signal(barrier, device):
    pl.semaphore_signal(barrier, inc=1, device_id=device, device_id_type=MESH)


def neighbours(n_row, n_col):
    row, col = lax.axis_index("row"), lax.axis_index("col")
    found = {}
    for dr in (-1, 0, 1):
        for dc in (-1, 0, 1):
            if dr == 0 and dc == 0:
                continue
            r, c = row + dr, col + dc
            exists = (r >= 0) & (r < n_row) & (c >= 0) & (c < n_col)
            found[dr, dc] = (exists, (r, c))
    return found


def shift_kernel(n_row, n_col, offsets, fractions, after, before_in, r_in, c_in, h_in, diff, partial, edges,
                 ends, flanks, slots, via, extra, own, before, r_tab, c_tab, h_tab, wide, mid,
                 send, recv, slot_send, slot_recv, via_send, via_recv, load):
    scans, height, length = after.shape
    near = neighbours(n_row, n_col)
    here = (lax.axis_index("row"), lax.axis_index("col"))
    loads = [
        pltpu.make_async_copy(src, dst, load.at[k])
        for k, (src, dst) in enumerate((
            (after, own), (before_in, before), (r_in.at[here[0]], r_tab),
            (c_in.at[here[1]], c_tab), (h_in.at[here[1]], h_tab),
        ))
    ]
    for copy in loads:
        copy.start()
    barrier = pltpu.get_barrier_semaphore()
    count = jnp.int32(0)
    for exists, device in near.values():
        count += exists.astype(jnp.int32)

        @pl.when(exists)
        def _():
            signal(barrier, device)

    row, col = lax.axis_index("row"), lax.axis_index("col")
    relayed = range(scans // 2, scans) if n_row == 8 else range(0)
    routes = {1: (3, 7, 4), -1: (4, 0, 3)}
    if relayed:
        for one, others in ((0, (3, 4)), (7, (3, 4)), (3, (0, 7)), (4, (0, 7))):
            count += jnp.where(row == one, 2, 0)

            @pl.when(row == one)
            def _():
                for other in others:
                    signal(barrier, (other, col))

    loads[0].wait()
    for s in range(scans):
        extra[s] = jnp.transpose(own[s, :, LANES : 2 * LANES])[0:8]
        extra[s, 7:8] = jnp.transpose(own[s, :, length - 2 * LANES : length - LANES])[LANES - 1 :]
    pl.semaphore_wait(barrier, count)

    def row_copy(s, dr):
        src = pl.ds(height - HALO, HALO) if dr == 1 else pl.ds(0, HALO)
        k = 0 if dr == 1 else 1
        return remote(
            after.at[s, src, :], ends.at[k, s, :, pl.ds(LANES, length)],
            send.at[k, s], recv.at[k, s], near[dr, 0][1],
        )

    def first_leg(s, dr):
        src = pl.ds(height - HALO, HALO) if dr == 1 else pl.ds(0, HALO)
        k = 0 if dr == 1 else 1
        return remote(
            after.at[s, src, :], via.at[s - relayed[0]],
            send.at[k, s], via_recv.at[s - relayed[0]], (routes[dr][1], col),
        )

    def second_leg(s, dr):
        k = 0 if dr == 1 else 1
        return remote(
            via.at[s - relayed[0]], ends.at[k, s, :, pl.ds(LANES, length)],
            via_send.at[s - relayed[0]], recv.at[k, s], (routes[dr][2], col),
        )

    def col_copy(s, dc, band):
        side = 0 if dc == 1 else 1
        k = 2 + (band + 1) * 2 + side
        first = length - LANES if dc == 1 else 0
        if band == 0:
            src, dst = after.at[s, :, pl.ds(first, LANES)], flanks.at[side, s]
        else:
            v = 0 if band == -1 else 1
            src = ends.at[v, s, :, pl.ds(LANES + first, LANES)]
            dst = ends.at[v, s, :, pl.ds(0 if dc == 1 else LANES + length, LANES)]
        return remote(src, dst, send.at[k, s], recv.at[k, s], near[0, dc][1])

    def slot_copy(dr, dc):
        k = (0 if dc == 1 else 3) + (1 - dr)
        return remote(extra, slots.at[k], slot_send.at[k], slot_recv.at[k], near[dr, dc][1])

    def when(pred, action):
        pl.when(pred)(action)

    for dc in (1, -1):
        for dr in (-1, 0, 1):
            when(near[dr, dc][0], slot_copy(dr, dc).start)
    for s in relayed:
        for dr in (1, -1):
            when(row == routes[dr][0], first_leg(s, dr).start)
    for s in range(scans):
        for dr in (1, -1):
            direct = near[dr, 0][0]
            if s in relayed:
                direct = direct & (row != routes[dr][0])
            when(direct, row_copy(s, dr).start)
    for s in range(scans):
        for dc in (1, -1):
            when(near[0, dc][0], col_copy(s, dc, 0).start)
    for s in relayed:
        for dr in (1, -1):
            when(row == routes[dr][1], first_leg(s, dr).wait_recv)
            when(row == routes[dr][1], second_leg(s, dr).start)
    for copy in loads[1:]:
        copy.wait()
    for dc in (1, -1):
        for dr in (-1, 0, 1):
            when(near[-dr, -dc][0], slot_copy(dr, dc).wait_recv)

    def step(t, carry):
        @pl.when(t < scans)
        def _():
            for dr in (1, -1):
                source = near[-dr, 0][0]
                when(source, row_copy(t, dr).wait_recv)
                for dc in (1, -1):
                    when(source & near[0, dc][0], col_copy(t, dc, -dr).start)

        @pl.when(t > 0)
        def _():
            for dc in (1, -1):
                for band in (-1, 0, 1):
                    ok = jnp.bool_(True) if band == 0 else near[band, 0][0]
                    when(ok & near[0, -dc][0], col_copy(t - 1, dc, band).wait_recv)
            shift_scan(
                n_row, n_col, t - 1, offsets, fractions, own, ends, flanks, before, slots, r_tab, c_tab, h_tab,
                diff, partial, edges, wide, mid,
            )

        return carry

    lax.fori_loop(0, scans + 1, step, 0)
    for s in range(scans):
        for dr in (1, -1):
            when(near[dr, 0][0], row_copy(s, dr).wait_send)
        for dc in (1, -1):
            for band in (-1, 0, 1):
                ok = jnp.bool_(True) if band == 0 else near[band, 0][0]
                when(ok & near[0, dc][0], col_copy(s, dc, band).wait_send)
    for s in relayed:
        for dr in (1, -1):
            when(row == routes[dr][1], second_leg(s, dr).wait_send)
    for dc in (1, -1):
        for dr in (-1, 0, 1):
            when(near[dr, dc][0], slot_copy(dr, dc).wait_send)


def split2(value):
    high = value.astype(BF16)
    return high, (value - high.astype(F32)).astype(BF16)


def cubic(t):
    t2 = t * t
    t3 = t2 * t
    return (
        0.5 * (2.0 * t2 - t3 - t),
        0.5 * (3.0 * t3 - 5.0 * t2 + 2.0),
        0.5 * (4.0 * t2 - 3.0 * t3 + t),
        0.5 * (t3 - t2),
    )


def shift_scan(n_row, n_col, s, offsets, fractions, after, ends, flanks, before, slots, r_tab, c_tab, h_tab,
               diff, partial, edges, wide, mid):
    scans, height, length = before.shape
    width = length + 2 * LANES
    dr, dc = offsets[0, 0, 0, s], offsets[1, 0, 0, s]
    rt = cubic(fractions[0, 0, 0, s].astype(F32) / 256.0)
    ct = cubic(fractions[1, 0, 0, s].astype(F32) / 256.0)
    col = lax.axis_index("col")
    zero = jnp.float32(0.0)
    row = lax.axis_index("row")
    has_left, has_right = col > 0, col < n_col - 1
    has_rows = (row > 0, jnp.bool_(True), row < n_row - 1)
    first, last = slice(0, LANES), slice(length + 3 * LANES, length + 4 * LANES)
    left, inner = slice(LANES, 2 * LANES), slice(2 * LANES, 2 * LANES + length)
    right = slice(2 * LANES + length, 3 * LANES + length)
    blank = jnp.zeros((LANES - 8, height), F32)
    spans = (
        (slice(0, HALO), slice(height - HALO, height)),
        (slice(HALO, HALO + height), slice(0, height)),
        (slice(HALO + height, height + 2 * HALO), slice(0, HALO)),
    )
    for j, (here, part) in enumerate(spans):
        low = jnp.transpose(jnp.concatenate([blank, slots[j, s]], axis=0))
        high = jnp.transpose(jnp.concatenate([slots[3 + j, s], blank], axis=0))
        wide[here, first] = jnp.where(has_left & has_rows[j], low[part], zero)
        wide[here, last] = jnp.where(has_right & has_rows[j], high[part], zero)
    for v in range(2):
        here = spans[2 * v][0]
        found = has_rows[2 * v]
        wide[here, left] = jnp.where(has_left & found, ends[v, s, :, 0:LANES], zero)
        wide[here, inner] = jnp.where(found, ends[v, s, :, LANES : LANES + length], zero)
        wide[here, right] = jnp.where(has_right & found, ends[v, s, :, LANES + length :], zero)
    here = spans[1][0]
    wide[here, left] = jnp.where(has_left, flanks[0, s], zero)
    wide[here, inner] = after[s]
    wide[here, right] = jnp.where(has_right, flanks[1, s], zero)
    def taps_at(shape, axis, offset, weights):
        tap = lax.broadcasted_iota(jnp.int32, shape, axis)
        tap = tap - lax.broadcasted_iota(jnp.int32, shape, 1 - axis) - offset
        taps = jnp.zeros(shape, F32)
        for b in range(4):
            taps = jnp.where(tap == b, weights[b], taps)
        return split2(taps)

    t_high, t_low = taps_at((height, height + 2 * HALO), 1, HALO - 1 + dr, rt)
    high, low = split2(wide[...])
    two = jnp.dot(jnp.concatenate([t_high, t_low], axis=0), high, preferred_element_type=F32)
    mid[...] = two[:height] + two[height:] + jnp.dot(t_high, low, preferred_element_type=F32)
    t_high, t_low = taps_at((6 * LANES, 2 * LANES), 0, 2 * LANES - 1 + dc, ct)
    high, low = split2(mid[...])
    both = jnp.concatenate([high, low], axis=0)
    for begin in range(0, length, 2 * LANES):
        window = slice(begin, begin + 6 * LANES)
        two = jnp.dot(both[:, window], t_high, preferred_element_type=F32)
        z = two[:height] + two[height:] + jnp.dot(
            high[:, window], t_low, preferred_element_type=F32
        )
        here = slice(begin, begin + 2 * LANES)
        diff[s, :, here] = before[s, :, here] - z
    high, low = split2(diff[s])
    rr = r_tab[...]
    pr = rr.shape[0] // 2
    both = jnp.dot(rr, high, preferred_element_type=F32)
    mixed = both[:pr] + both[pr:] + jnp.dot(rr[:pr], low, preferred_element_type=F32)
    here = jnp.dot(mixed, c_tab[...], precision=HIGHEST, preferred_element_type=F32)
    for t in range(partial.shape[0]):
        partial[t, s] = jnp.dot(here, h_tab[t], precision=HIGHEST, preferred_element_type=F32)
    edges[s, 0:EDGE] = jnp.transpose(diff[s, :, 0:LANES])[0:EDGE]
    edges[s, EDGE:] = jnp.transpose(diff[s, :, length - LANES :])[LANES - EDGE :]


def gather_kernel(n_row, n_col, diff, partial, edges, rows_out, corners, sides, spread, parts,
                  psend, precv, qsend, qrecv, nsend, nrecv):
    scans, height, length = diff.shape
    near = neighbours(n_row, n_col)
    row, col = lax.axis_index("row"), lax.axis_index("col")
    barrier = pltpu.get_barrier_semaphore()
    count = jnp.int32(n_row - 1 + n_col - 1)
    for k in range(1, n_col):
        signal(barrier, (row, lax.rem(col + k, n_col)))
    for k in range(1, n_row):
        signal(barrier, (lax.rem(row + k, n_row), col))
    for (dr, dc), (exists, device) in near.items():
        if dr and dc:
            count += exists.astype(jnp.int32)

            @pl.when(exists)
            def _():
                signal(barrier, device)

    pl.semaphore_wait(barrier, count)

    def p_copy(k):
        target = lax.rem(col + k, n_col)
        return remote(
            partial.at[target], parts.at[col], psend.at[k - 1], precv.at[k - 1], (row, target)
        )

    def q_copy(k):
        return remote(
            spread.at[row], spread.at[row], qsend.at[k - 1], qrecv.at[k - 1],
            (lax.rem(row + k, n_row), col),
        )

    def near_copy(dr, dc):
        device = near[dr, dc][1]
        vertical = pl.ds(height - EDGE, EDGE) if dr == 1 else pl.ds(0, EDGE)
        k = (dr + 1) * 3 + dc + 1
        v = 0 if dr == 1 else 1
        if dc == 0:
            src, dst = diff.at[:, vertical, :], rows_out.at[v]
        elif dr == 0:
            src = edges.at[:, pl.ds(EDGE if dc == 1 else 0, EDGE), :]
            dst = sides.at[0 if dc == 1 else 1]
        else:
            lanes = pl.ds(length - LANES, LANES) if dc == 1 else pl.ds(0, LANES)
            src = diff.at[:, vertical, lanes]
            dst = corners.at[v * 2 + (0 if dc == 1 else 1)]
        return remote(src, dst, nsend.at[k], nrecv.at[k], device)

    for k in range(1, n_col):
        p_copy(k).start()
    for (dr, dc), (exists, _) in near.items():
        pl.when(exists)(near_copy(dr, dc).start)
    own = partial[col]
    for k in range(1, n_col):
        p_copy(k).wait_recv()
        own = own + parts[lax.rem(col - k + n_col, n_col)]
    spread[row] = own
    for k in range(1, n_row):
        q_copy(k).start()
    for k in range(1, n_col):
        p_copy(k).wait_send()
    for (dr, dc), (exists, _) in near.items():
        pl.when(exists)(near_copy(dr, dc).wait_send)
        pl.when(near[-dr, -dc][0])(near_copy(dr, dc).wait_recv)
    for k in range(1, n_row):
        q_copy(k).wait_send()
        q_copy(k).wait_recv()


def band_kernel(n_row, n_col, place, diff, rows_in, corners, sides, spread, ru, cu, cw, gc, gr,
                band_out, slope_out, sums, x, b):
    row, col = place[0], place[1]
    height, length = diff.shape[1], diff.shape[2]
    width = length + 2 * LANES
    tall = height + 2 * EDGE
    zero = jnp.float32(0.0)
    has_top, has_bottom = row > 0, row < n_row - 1
    row = lax.axis_index("row")
    has_left, has_right = col > 0, col < n_col - 1
    has_rows = (row > 0, jnp.bool_(True), row < n_row - 1)
    mid = slice(LANES, LANES + length)
    x[EDGE : EDGE + height, mid] = diff[0]
    x[0:EDGE, mid] = jnp.where(has_top, rows_in[0, 0], zero)
    x[EDGE + height :, mid] = jnp.where(has_bottom, rows_in[1, 0], zero)
    x[0:EDGE, 0:LANES] = jnp.where(has_top & has_left, corners[0, 0], zero)
    x[0:EDGE, LANES + length :] = jnp.where(has_top & has_right, corners[1, 0], zero)
    x[EDGE + height :, 0:LANES] = jnp.where(has_bottom & has_left, corners[2, 0], zero)
    x[EDGE + height :, LANES + length :] = jnp.where(has_bottom & has_right, corners[3, 0], zero)
    blank = jnp.zeros((LANES - EDGE, height), F32)
    left = jnp.where(has_left, sides[0, 0], zero)
    right = jnp.where(has_right, sides[1, 0], zero)
    x[EDGE : EDGE + height, 0:LANES] = jnp.transpose(jnp.concatenate([blank, left], axis=0))
    x[EDGE : EDGE + height, LANES + length :] = jnp.transpose(
        jnp.concatenate([right, blank], axis=0)
    )

    high, low = split2(x[...])
    both = jnp.concatenate([high, low], axis=0)
    pieces = []
    for first in range(0, width, 2 * LANES):
        begin, end = max(first - LANES, 0), min(first + 3 * LANES, width)
        skip = begin - (first - LANES)
        g_high = gc[0, skip : skip + end - begin, :]
        g_low = gc[0, 4 * LANES + skip : 4 * LANES + skip + end - begin, :]
        two = jnp.dot(both[:, begin:end], g_high, preferred_element_type=F32)
        pieces.append(
            two[:tall] + two[tall:]
            + jnp.dot(high[:, begin:end], g_low, preferred_element_type=F32)
        )
    high, low = split2(jnp.concatenate(pieces, axis=1) * cw[0])
    two = jnp.dot(gr[0], high, preferred_element_type=F32)
    smooth = two[:tall] + two[tall:] + jnp.dot(gr[0, :tall], low, preferred_element_type=F32)
    q = jnp.concatenate([spread[i, 0] for i in range(n_row)], axis=0)
    mixed = jnp.dot(ru[0], q, precision=HIGHEST, preferred_element_type=F32)
    pieces = jnp.concatenate(split2(mixed), axis=1)
    cub = cu[0].astype(BF16)
    wavy = jnp.dot(pieces, jnp.concatenate([cub, cub], axis=0), preferred_element_type=F32)
    b[...] = smooth - wavy

    lane = lax.broadcasted_iota(jnp.int32, (1, length), 1) + col * length
    col_mask = ((lane >= 1) & (lane <= n_col * length - 2)).astype(F32)

    def slope(r, carry):
        base = pl.multiple_of(r * 8, 8)
        v = b[pl.ds(base, 24), :]
        center = v[8:16]
        gc = (pltpu.roll(center, width - 1, 1) - pltpu.roll(center, 1, 1))[:, mid] * col_mask
        index = lax.broadcasted_iota(jnp.int32, (8, 1), 0) + row * height + base
        row_mask = ((index >= 1) & (index <= n_row * height - 2)).astype(F32)
        gr = (v[9:17, mid] - v[7:15, mid]) * row_mask
        value = gc * gc + gr * gr
        field = center[:, mid]
        here = pl.ds(base, 8)
        band_out[0, here, :] = field
        slope_out[0, here, :] = value
        return carry[0] + field * field, carry[1] + value

    start = jnp.zeros((8, length), F32)
    heights, slopes = lax.fori_loop(0, height // 8, slope, (start, start), unroll=2)
    sums[0, 0] = sum(heights[:, i : i + LANES] for i in range(0, length, LANES))
    sums[0, 1] = sum(slopes[:, i : i + LANES] for i in range(0, length, LANES))


def total_kernel(n_row, n_col, cells, sums, out, held, parts, psend, precv, qsend, qrecv):
    row, col = lax.axis_index("row"), lax.axis_index("col")
    scans = sums.shape[0]
    barrier = pltpu.get_barrier_semaphore()
    for k in range(1, n_col):
        signal(barrier, (row, lax.rem(col + k, n_col)))
    for k in range(1, n_row):
        signal(barrier, (lax.rem(row + k, n_row), col))
    for k in range(2):
        for s in range(scans):
            held[0, k * scans + s : k * scans + s + 1] = jnp.sum(sums[s, k], axis=0, keepdims=True)
    pl.semaphore_wait(barrier, n_row + n_col - 2)

    def p_copy(k):
        return remote(
            held.at[0], parts.at[k - 1], psend.at[k - 1], precv.at[k - 1],
            (row, lax.rem(col + k, n_col)),
        )

    def q_copy(k):
        slot = n_col - 1 + k - 1
        return remote(
            held.at[1], parts.at[slot], qsend.at[k - 1], qrecv.at[k - 1],
            (lax.rem(row + k, n_row), col),
        )

    for k in range(1, n_col):
        p_copy(k).start()
    value = held[0]
    for k in range(1, n_col):
        p_copy(k).wait_recv()
        value = value + parts[k - 1]
    held[1] = value
    for k in range(1, n_row):
        q_copy(k).start()
    for k in range(1, n_row):
        q_copy(k).wait_recv()
        value = value + parts[n_col - 1 + k - 1]
    result = jnp.sqrt(jnp.sum(value, axis=1, keepdims=True) / cells + EPSILON)
    spread = jnp.broadcast_to(result, value.shape)
    index = lax.broadcasted_iota(jnp.int32, value.shape, 0)
    lane = lax.broadcasted_iota(jnp.int32, value.shape, 1)
    for k in range(2):
        picked = jnp.sum(jnp.where(index == k * scans + lane, spread, 0.0), axis=0, keepdims=True)
        out[k : k + 1, :] = picked[:, 0:scans]
    for k in range(1, n_col):
        p_copy(k).wait_send()
    for k in range(1, n_row):
        q_copy(k).wait_send()


def body(n_row, n_col, before, after, offsets, fractions):
    scans, height, length = before.shape
    width = length + 2 * LANES
    tall = height + 2 * EDGE
    c_tab, hc, cu, ru, cw, r_tab, gc, gr = tables(n_row * height, n_col * length, height, length)
    pr = r_tab.shape[1] // 2
    place = jnp.stack([lax.axis_index("row"), lax.axis_index("col")]).astype(jnp.int32)
    struct = jax.ShapeDtypeStruct
    dma = pltpu.SemaphoreType.DMA
    smem = pl.BlockSpec(memory_space=pltpu.SMEM)
    scan_last = (0, 2, 3, 1)
    diff, partial, edges = pl.pallas_call(
        functools.partial(shift_kernel, n_row, n_col),
        out_shape=(
            struct((scans, height, length), F32),
            struct((n_col, scans, pr, LANES), F32),
            struct((scans, 2 * EDGE, height), F32),
        ),
        in_specs=[smem, smem, ANY, ANY, ANY, ANY, ANY],
        out_specs=(VM, VM, VM),
        scratch_shapes=[
            pltpu.VMEM((2, scans, HALO, width), F32),
            pltpu.VMEM((2, scans, height, LANES), F32),
            pltpu.VMEM((6, scans, 8, height), F32),
            pltpu.VMEM((scans - scans // 2, HALO, length), F32),
            pltpu.VMEM((scans, 8, height), F32),
            pltpu.VMEM((scans, height, length), F32),
            pltpu.VMEM((scans, height, length), F32),
            pltpu.VMEM(r_tab.shape[1:], BF16),
            pltpu.VMEM(c_tab.shape[1:], F32),
            pltpu.VMEM(hc.shape[1:], F32),
            pltpu.VMEM((height + 2 * HALO, width + 2 * LANES), F32),
            pltpu.VMEM((height, width + 2 * LANES), F32),
            dma((8, scans)), dma((8, scans)), dma((6,)), dma((6,)), dma((scans,)), dma((scans,)),
            dma((5,)),
        ],
        compiler_params=pltpu.CompilerParams(
            collective_id=0, has_side_effects=True, vmem_limit_bytes=VMEM_LIMIT
        ),
        name="shift",
    )(offsets.transpose(scan_last), fractions.transpose(scan_last), after, before, r_tab, c_tab, hc)

    all_scan = lambda s, *_: (0, s, 0, 0)
    by_scan = lambda s, *_: (s, 0, 0)
    row_part = lambda s, p, *_: (p[0], 0, 0)
    col_part = lambda s, p, *_: (p[1], 0, 0)
    rows_out, corners, sides, spread = pl.pallas_call(
        functools.partial(gather_kernel, n_row, n_col),
        out_shape=(
            struct((2, scans, EDGE, length), F32),
            struct((4, scans, EDGE, LANES), F32),
            struct((2, scans, EDGE, height), F32),
            struct((n_row, scans, pr, LANES), F32),
        ),
        in_specs=[ANY, VM, VM],
        out_specs=(VM, VM, VM, VM),
        scratch_shapes=[
            pltpu.VMEM((n_col, scans, pr, LANES), F32),
            dma((n_col - 1,)), dma((n_col - 1,)), dma((n_row - 1,)), dma((n_row - 1,)),
            dma((9,)), dma((9,)),
        ],
        compiler_params=pltpu.CompilerParams(
            collective_id=1, has_side_effects=True, vmem_limit_bytes=VMEM_LIMIT
        ),
        name="gather",
    )(diff, partial, edges)

    band, slope, sums = pl.pallas_call(
        functools.partial(band_kernel, n_row, n_col),
        out_shape=(
            struct((scans, height, length), F32),
            struct((scans, height, length), F32),
            struct((scans, 2, 8, LANES), F32),
        ),
        grid_spec=pltpu.PrefetchScalarGridSpec(
            num_scalar_prefetch=1,
            grid=(scans,),
            in_specs=[
                pl.BlockSpec((1, height, length), by_scan),
                pl.BlockSpec((2, 1, EDGE, length), all_scan),
                pl.BlockSpec((4, 1, EDGE, LANES), all_scan),
                pl.BlockSpec((2, 1, EDGE, height), all_scan),
                pl.BlockSpec((n_row, 1, pr, LANES), all_scan),
                pl.BlockSpec((1, tall, n_row * pr), row_part),
                pl.BlockSpec((1, LANES, width), col_part),
                pl.BlockSpec((1, 1, width), col_part),
                pl.BlockSpec((1, 8 * LANES, 2 * LANES), lambda s, *_: (0, 0, 0)),
                pl.BlockSpec((1, 2 * tall, tall), row_part),
            ],
            out_specs=(
                pl.BlockSpec((1, height, length), by_scan),
                pl.BlockSpec((1, height, length), by_scan),
                pl.BlockSpec((1, 2, 8, LANES), lambda s, *_: (s, 0, 0, 0)),
            ),
            scratch_shapes=[pltpu.VMEM((tall, width), F32)] * 2,
        ),
        compiler_params=pltpu.CompilerParams(vmem_limit_bytes=VMEM_LIMIT),
        name="band",
    )(place, diff, rows_out, corners, sides, spread, ru, cu, cw, gc, gr)
    params = pl.pallas_call(
        functools.partial(total_kernel, n_row, n_col, float(n_row * height * n_col * length)),
        out_shape=struct((2, scans), F32),
        in_specs=[VM],
        out_specs=VM,
        scratch_shapes=[
            pltpu.VMEM((2, 2 * scans, LANES), F32),
            pltpu.VMEM((n_row + n_col - 2, 2 * scans, LANES), F32),
            dma((n_col - 1,)), dma((n_col - 1,)), dma((n_row - 1,)), dma((n_row - 1,)),
        ],
        compiler_params=pltpu.CompilerParams(collective_id=2, has_side_effects=True),
        name="total",
    )(sums)
    return band, slope, params


def solution(mesh):
    n_row, n_col = mesh.shape["row"], mesh.shape["col"]
    spec = P(None, "row", "col")
    small = P(None, None, "row", "col")
    return jax.shard_map(
        functools.partial(body, n_row, n_col),
        mesh=mesh,
        in_specs=(spec, spec, small, small),
        out_specs=(spec, spec, P()),
        check_vma=False,
    )
```
